128 devices in a mesh: dp: 32 (over z, x, core), section: 4 (over y).
Axes of the slice: x: 4, y: 4, z: 4, core: 2. Of those that a mesh axis runs over, the one named last changes fastest.
Arguments:
- teacher_logits: bfloat16 [4096, 65536], P('dp', 'section'), may hold values from -1 to 1
- prototypes: bfloat16 [65536, 256], P('section'), may hold values from -0.3984375 to 0.3984375
- head_weight: bfloat16 [1536, 256], replicated, may hold values from -0.15625 to 0.15625
- student_out: bfloat16 [4096, 1536], P('dp'), may hold values from -6 to 6
- block_inputs: bfloat16 [4, 4096, 1536], P('section', 'dp'), may hold values from -6 to 6
- ln_gain: float32 [4, 1536], P('section'), may hold values from 0.25 to 1.75
- w_gate: bfloat16 [4, 1536, 2048], P('section', 'dp'), may hold values from -0.15625 to 0.15625
- w_up: bfloat16 [4, 1536, 2048], P('section', 'dp'), may hold values from -0.15625 to 0.15625
- w_down: bfloat16 [4, 2048, 1536], P('section', 'dp'), may hold values from -0.125 to 0.125
Outputs:
- grad_in: bfloat16 [4, 4096, 1536], P('section', 'dp')
The draws below stay inside these ranges and needn't reach their ends.
All inputs are finite; a program needn't handle non-finite values.
Results may differ from the reference program's by a relative error of at most 0.022.
Values may be sent and summed in bfloat16 or wider, within the bound.
No kernel may reach another device: no remote copies, remote signals or barrier semaphores. Data moves between devices by JAX's collectives and lax.ppermute only.
A program may use at most 128 MiB of HBM per device.

```python
import math
import jax
import jax.numpy as jnp
from jax import lax

D = 1536
H = 2048
K = 65536
BOT = 256
N_ITER = 3
B = 4096
N_SECTION = 4


def crop_preference(key, noise_scale, margin, wave_scale):
    noise_key, phase_key, crop_key, column_key = jax.random.split(key, 4)
    noise = jax.random.uniform(noise_key, (B, K), jnp.float32, -1.0, 1.0)
    phase = jax.random.uniform(phase_key, (B, 1), jnp.float32)
    position = jnp.arange(K, dtype=jnp.float32)[None, :] / K
    wave = jnp.cos(2.0 * math.pi * (position + phase))
    crop_draw = jax.random.randint(crop_key, (B, 1), 0, 16)
    crop_group = (crop_draw >= 8).astype(jnp.int32) + (crop_draw >= 12).astype(jnp.int32) + (crop_draw >= 14).astype(jnp.int32)
    column_draw = jax.random.randint(column_key, (1, K), 0, 16)
    column_group = (column_draw >= 2).astype(jnp.int32) + (column_draw >= 4).astype(jnp.int32) + (column_draw >= 8).astype(jnp.int32)
    preferred = jnp.where(crop_group == column_group, 0.5 * margin, -0.5 * margin)
    return noise_scale * noise + preferred + wave_scale * wave


def draw_teacher_logits(key, part):
    key = jax.random.fold_in(key, 11)
    values = crop_preference(key, 0.4, 0.5, 0.1)
    return values.astype(jnp.bfloat16)


def levels(own_key, shape, shards, smallest, top_value):
    def one(dim, parts):
        draws = jax.random.uniform(jax.random.fold_in(jax.random.fold_in(own_key, 6), dim), (parts,), jnp.float32, smallest / len(shards), top_value / len(shards))
        return jnp.repeat(jnp.exp(draws), shape[dim] // parts).reshape((-1,) + (1,) * (len(shape) - dim - 1))

    level = one(*shards[0])
    for cut in shards[1:]:
        level = level * one(*cut)
    return level


def normal_values(key, shape, scale, reach, shards=(), kind=jnp.bfloat16):
    array = scale * jax.random.normal(key, shape, jnp.float32)
    if shards:
        array = array * levels(key, shape, shards, -0.22, 0.18)
    return jnp.clip(array, -reach, reach).astype(kind)


def setup_inputs(seed: int = 0) -> dict:
    keys = jax.random.split(jax.random.key(seed), 10)
    teacher_logits = draw_teacher_logits(jax.random.fold_in(keys[9], 71), 0)
    prototypes = jnp.clip(jax.random.uniform(keys[1], (K, BOT), jnp.float32, -0.3984375, 0.3984375) * levels(keys[1], (K, BOT), ((0, 4),), -0.4, 0.0), -0.3984375, 0.3984375).astype(jnp.bfloat16)
    head_weight = normal_values(keys[2], (D, BOT), D ** -0.5, 0.15625)
    student_out = normal_values(keys[3], (B, D), 1.0, 6.0, ((0, 32),))
    block_inputs = normal_values(keys[4], (N_SECTION, B, D), 1.0, 6.0, ((0, 4), (1, 32)))
    ln_gain = jnp.clip(1.0 + 0.15 * jax.random.normal(keys[5], (N_SECTION, D), jnp.float32), 0.25, 1.75)
    w_gate = normal_values(keys[6], (N_SECTION, D, H), D ** -0.5, 0.15625, ((0, 4), (1, 32)))
    w_up = normal_values(keys[7], (N_SECTION, D, H), D ** -0.5, 0.15625, ((0, 4), (1, 32)))
    w_down = normal_values(keys[8], (N_SECTION, H, D), H ** -0.5, 0.125, ((0, 4), (1, 32)))
    return {"teacher_logits": teacher_logits, "prototypes": prototypes, "head_weight": head_weight, "student_out": student_out, "block_inputs": block_inputs, "ln_gain": ln_gain, "w_gate": w_gate, "w_up": w_up, "w_down": w_down}


teacher_temp = 0.07
student_temp = 0.1
epsilon = 1e-06

def block_backward(block_in, grad_out, norm_gain, gate_weight, up_weight, down_weight):
    xfloat = block_in.astype(jnp.float32)
    middle = lax.optimization_barrier(jnp.mean(xfloat, axis=1, keepdims=True))
    centered_rows = xfloat - middle
    inverse_deviation = lax.rsqrt(lax.optimization_barrier(jnp.mean(centered_rows * centered_rows, axis=1, keepdims=True)) + epsilon)
    normalized_input = centered_rows * inverse_deviation
    normed_input = (normalized_input * norm_gain[None, :]).astype(jnp.bfloat16)
    gate = jnp.dot(normed_input, gate_weight, preferred_element_type=jnp.float32)
    upper = jnp.dot(normed_input, up_weight, preferred_element_type=jnp.float32)
    sigma = jax.nn.sigmoid(gate)
    dmid = jnp.dot(grad_out, down_weight.T, preferred_element_type=jnp.float32)
    dgate = (dmid * upper * sigma * (1.0 + gate * (1.0 - sigma))).astype(jnp.bfloat16)
    dupper = (dmid * gate * sigma).astype(jnp.bfloat16)
    dnormed = jnp.dot(dgate, gate_weight.T, preferred_element_type=jnp.float32) + jnp.dot(dupper, up_weight.T, preferred_element_type=jnp.float32)
    normalized_gradient = dnormed * norm_gain[None, :]
    inner_product = normalized_gradient - lax.optimization_barrier(jnp.mean(normalized_gradient, axis=1, keepdims=True)) - normalized_input * lax.optimization_barrier(jnp.mean(normalized_gradient * normalized_input, axis=1, keepdims=True))
    return (grad_out.astype(jnp.float32) + inverse_deviation * inner_product).astype(jnp.bfloat16)

def reference(teacher_logits, prototypes, head_weight, student_out, block_inputs, ln_gain, w_gate, w_up, w_down):
    weights = jnp.exp(teacher_logits.astype(jnp.float32) / teacher_temp)
    for step in range(N_ITER):
        weights = weights / lax.optimization_barrier(jnp.sum(weights, axis=0, keepdims=True))
        weights = weights / lax.optimization_barrier(jnp.sum(weights, axis=1, keepdims=True))
    targets = lax.optimization_barrier(weights.astype(jnp.bfloat16)).astype(jnp.float32)
    feature = jnp.dot(student_out, head_weight, preferred_element_type=jnp.float32)
    radius = jnp.sqrt(lax.optimization_barrier(jnp.sum(feature * feature, axis=1, keepdims=True)) + epsilon)
    unit = feature / radius
    scores = jnp.dot(unit.astype(jnp.bfloat16), prototypes.T, preferred_element_type=jnp.float32)
    expo = jnp.exp(scores / student_temp)
    total = lax.optimization_barrier(jnp.sum(expo, axis=1, keepdims=True))
    dscore = ((expo / total - targets) / student_temp).astype(jnp.bfloat16)
    dunit = jnp.dot(dscore, prototypes, preferred_element_type=jnp.float32)
    dfeature = ((dunit - unit * lax.optimization_barrier(jnp.sum(unit * dunit, axis=1, keepdims=True))) / radius).astype(jnp.bfloat16)
    grad = jnp.dot(dfeature, head_weight.T, preferred_element_type=jnp.float32).astype(jnp.bfloat16)
    results = []
    for section in reversed(range(N_SECTION)):
        grad = block_backward(block_inputs[section], grad, ln_gain[section], w_gate[section], w_up[section], w_down[section])
        results.insert(0, grad)
    return jnp.stack(results)
```

```python
import jax
import jax.numpy as jnp
from jax import lax
from jax.experimental import pallas as pl
from jax.experimental.pallas import tpu as pltpu
from jax.sharding import PartitionSpec as P

TEACHER_SCALE = 1.0 / 0.07
STUDENT_SCALE = 1.0 / 0.1
EPS = 1e-06
N_ITER = 3
F32 = jnp.float32
BF16 = jnp.bfloat16
NT = (((1,), (1,)), ((), ()))
VMEM_LIMIT = 48 * 1024 * 1024
SHAPE = jax.ShapeDtypeStruct


def params():
    return pltpu.CompilerParams(vmem_limit_bytes=VMEM_LIMIT, dimension_semantics=("arbitrary",))


def cost(flops, size, transcendentals=0):
    return pl.CostEstimate(flops=flops, bytes_accessed=size, transcendentals=transcendentals)


def whole(shape):
    return pl.BlockSpec(shape, lambda j: (0,) * len(shape))


def row_to_column(row):
    n = row.shape[1]
    eye = lax.broadcasted_iota(jnp.int32, (n, n), 0) == lax.broadcasted_iota(jnp.int32, (n, n), 1)
    return jnp.sum(jnp.where(eye, row, 0.0), axis=1, keepdims=True)


def column_to_row(column):
    n = column.shape[0]
    eye = lax.broadcasted_iota(jnp.int32, (n, n), 0) == lax.broadcasted_iota(jnp.int32, (n, n), 1)
    return jnp.sum(jnp.where(eye, column, 0.0), axis=0, keepdims=True)


def teacher_weights(logits):
    return jnp.exp(logits.astype(F32) * TEACHER_SCALE)


def column_sums(logits, row_parts, width=4096):
    rows, columns = logits.shape

    def kernel(l_ref, *refs):
        out_ref = refs[-1]
        weights = teacher_weights(l_ref[...])
        if len(refs) > 1:
            sums = refs[0][...]
            for ref in refs[1:-1]:
                sums = sums + ref[...]
            weights = weights * row_to_column(1.0 / sums)
        out_ref[...] = jnp.sum(weights, axis=0, keepdims=True)

    return pl.pallas_call(
        kernel,
        grid=(columns // width,),
        in_specs=[pl.BlockSpec((rows, width), lambda j: (0, j))] + [whole((1, rows))] * len(row_parts),
        out_specs=pl.BlockSpec((1, width), lambda j: (0, j)),
        out_shape=SHAPE((1, columns), F32),
        compiler_params=params(),
        cost_estimate=cost(4 * rows * columns, 2 * rows * columns, rows * columns),
        name="column_sums",
    )(logits, *row_parts)


def row_sums(logits, column_parts, width=4096):
    rows, columns = logits.shape

    def kernel(l_ref, *refs):
        out_ref, total = refs[-2:]
        step = pl.program_id(0)

        @pl.when(step == 0)
        def _():
            total[...] = jnp.zeros_like(total)

        sums = refs[0][...]
        for ref in refs[1:-2]:
            sums = sums + ref[...]
        scaled = teacher_weights(l_ref[...]) * (1.0 / sums)
        total[...] += jnp.sum(scaled, axis=1, keepdims=True)

        @pl.when(step == pl.num_programs(0) - 1)
        def _():
            out_ref[...] = column_to_row(total[...])

    return pl.pallas_call(
        kernel,
        grid=(columns // width,),
        in_specs=[pl.BlockSpec((rows, width), lambda j: (0, j))]
        + [pl.BlockSpec((1, width), lambda j: (0, j))] * len(column_parts),
        out_specs=whole((1, rows)),
        out_shape=SHAPE((1, rows), F32),
        scratch_shapes=[pltpu.VMEM((rows, 1), F32)],
        compiler_params=params(),
        cost_estimate=cost(4 * rows * columns, 2 * rows * columns, rows * columns),
        name="row_sums",
    )(logits, *column_parts)


def target_products(logits, column_parts, prototypes, width=2048):
    rows, columns = logits.shape
    bottleneck = prototypes.shape[1]

    def kernel(l_ref, p_ref, *refs):
        out_ref, total = refs[-2:]
        step = pl.program_id(0)

        @pl.when(step == 0)
        def _():
            out_ref[...] = jnp.zeros_like(out_ref)
            total[...] = jnp.zeros_like(total)

        sums = refs[0][...]
        for ref in refs[1:-2]:
            sums = sums + ref[...]
        scaled = teacher_weights(l_ref[...]) * (1.0 / sums)
        total[...] += jnp.sum(scaled, axis=1, keepdims=True)
        out_ref[:, :bottleneck] += jnp.dot(scaled.astype(BF16), p_ref[...], preferred_element_type=F32)

        @pl.when(step == pl.num_programs(0) - 1)
        def _():
            out_ref[:, bottleneck:] = jnp.broadcast_to(total[...], (rows, 128))

    return pl.pallas_call(
        kernel,
        grid=(columns // width,),
        in_specs=[
            pl.BlockSpec((rows, width), lambda j: (0, j)),
            pl.BlockSpec((width, bottleneck), lambda j: (j, 0)),
        ]
        + [pl.BlockSpec((1, width), lambda j: (0, j))] * len(column_parts),
        out_specs=whole((rows, bottleneck + 128)),
        out_shape=SHAPE((rows, bottleneck + 128), F32),
        scratch_shapes=[pltpu.VMEM((rows, 1), F32)],
        compiler_params=params(),
        cost_estimate=cost(2 * rows * columns * bottleneck, 12 * 1024 * 1024, rows * columns),
        name="target_products",
    )(logits, prototypes, *column_parts)


def student_products(student_out, head, prototypes, width=2048):
    rows, model = student_out.shape
    columns, bottleneck = prototypes.shape

    def kernel(s_ref, h_ref, p_ref, out_ref, unit_ref, radius_ref, unit_b, total):
        step = pl.program_id(0)

        @pl.when(step == 0)
        def _():
            feature = jnp.dot(s_ref[...], h_ref[...], preferred_element_type=F32)
            radius = jnp.sqrt(jnp.sum(feature * feature, axis=1, keepdims=True) + EPS)
            unit = feature / radius
            unit_ref[...] = unit
            radius_ref[...] = jnp.broadcast_to(radius, radius_ref.shape)
            unit_b[...] = unit.astype(BF16)
            out_ref[...] = jnp.zeros_like(out_ref)
            total[...] = jnp.zeros_like(total)

        block = p_ref[...]
        scores = lax.dot_general(unit_b[...], block, NT, preferred_element_type=F32)
        expo = jnp.exp(scores * STUDENT_SCALE)
        total[...] += jnp.sum(expo, axis=1, keepdims=True)
        out_ref[:, :bottleneck] += jnp.dot(expo.astype(BF16), block, preferred_element_type=F32)

        @pl.when(step == pl.num_programs(0) - 1)
        def _():
            out_ref[:, bottleneck:] = jnp.broadcast_to(total[...], (rows, 128))

    return pl.pallas_call(
        kernel,
        grid=(columns // width,),
        in_specs=[
            whole((rows, model)),
            whole((model, bottleneck)),
            pl.BlockSpec((width, bottleneck), lambda j: (j, 0)),
        ],
        out_specs=[whole((rows, bottleneck + 128)), whole((rows, bottleneck)), whole((rows, 128))],
        out_shape=[
            SHAPE((rows, bottleneck + 128), F32),
            SHAPE((rows, bottleneck), F32),
            SHAPE((rows, 128), F32),
        ],
        scratch_shapes=[pltpu.VMEM((rows, bottleneck), BF16), pltpu.VMEM((rows, 1), F32)],
        compiler_params=params(),
        cost_estimate=cost(4 * rows * columns * bottleneck, 8 * 1024 * 1024, rows * columns),
        name="student_products",
    )(student_out, head, prototypes)


def head_gradient(student_parts, target_parts, unit, radius, head):
    rows, bottleneck = unit.shape
    model = head.shape[0]
    count = len(student_parts)

    def kernel(*refs):
        unit_ref, radius_ref, h_ref, out_ref = refs[2 * count :]
        student = refs[0][...]
        for ref in refs[1:count]:
            student = student + ref[...]
        target = refs[count][...]
        for ref in refs[count + 1 : 2 * count]:
            target = target + ref[...]
        dunit = (
            student[:, :bottleneck] / student[:, bottleneck : bottleneck + 1]
            - target[:, :bottleneck] / target[:, bottleneck : bottleneck + 1]
        ) * STUDENT_SCALE
        unit = unit_ref[...]
        along = jnp.sum(unit * dunit, axis=1, keepdims=True)
        dfeature = ((dunit - unit * along) / radius_ref[:, :1]).astype(BF16)
        out_ref[...] = lax.dot_general(dfeature, h_ref[...], NT, preferred_element_type=F32).astype(BF16)

    parts = list(student_parts) + list(target_parts)
    return pl.pallas_call(
        kernel,
        out_shape=SHAPE((rows, model), BF16),
        compiler_params=pltpu.CompilerParams(vmem_limit_bytes=VMEM_LIMIT),
        cost_estimate=cost(2 * rows * model * bottleneck, 3 * 1024 * 1024),
        name="head_gradient",
    )(*parts, unit, radius, head)


def normalize(block_in):
    xfloat = block_in.astype(F32)
    centered = xfloat - jnp.mean(xfloat, axis=1, keepdims=True)
    inverse = lax.rsqrt(jnp.mean(centered * centered, axis=1, keepdims=True) + EPS)
    return centered * inverse, inverse


def pack_weights(w_gate, w_up, w_down, lanes):
    parts = []
    for w in (w_gate, w_up, w_down):
        parts += [w[:, k : k + lanes] for k in range(0, w.shape[1], lanes)]
    return jnp.concatenate(parts, axis=0)


def block_forward(block_in, gain, packed, shard_rows, hidden):
    rows, model = block_in.shape
    devices, _, lanes = packed.shape
    steps = hidden // lanes

    def kernel(x_ref, gain_ref, gate_ref, up_ref, a_ref, b_ref, normed):
        @pl.when(pl.program_id(0) == 0)
        def _():
            xhat, _ = normalize(x_ref[...])
            normed[...] = (xhat * gain_ref[...]).astype(BF16)

        z = normed[...]
        gate = jnp.dot(z, gate_ref[...].reshape(model, lanes), preferred_element_type=F32)
        up = jnp.dot(z, up_ref[...].reshape(model, lanes), preferred_element_type=F32)
        sigma = 1.0 / (1.0 + jnp.exp(-gate))
        a_ref[...] = up * sigma * (1.0 + gate * (1.0 - sigma))
        b_ref[...] = gate * sigma

    return pl.pallas_call(
        kernel,
        grid=(steps,),
        in_specs=[
            whole((rows, model)),
            whole((1, model)),
            pl.BlockSpec((devices, shard_rows, lanes), lambda j: (0, j, 0)),
            pl.BlockSpec((devices, shard_rows, lanes), lambda j: (0, steps + j, 0)),
        ],
        out_specs=[pl.BlockSpec((rows, lanes), lambda j: (0, j))] * 2,
        out_shape=[SHAPE((rows, hidden), F32)] * 2,
        scratch_shapes=[pltpu.VMEM((rows, model), BF16)],
        compiler_params=params(),
        cost_estimate=cost(4 * rows * model * hidden, 4 * model * hidden, rows * hidden),
        name="block_forward",
    )(block_in, gain, packed, packed)


def block_backward(grad, gate_factor, up_factor, block_in, gain, packed, shard_rows, down_rows):
    rows, model = block_in.shape
    hidden = gate_factor.shape[1]
    devices, _, lanes = packed.shape
    steps = hidden // lanes
    chunks = model // lanes
    holders = lanes // down_rows

    def kernel(g_ref, a_ref, b_ref, x_ref, gain_ref, gate_ref, up_ref, down_ref, out_ref, dz):
        step = pl.program_id(0)

        @pl.when(step == 0)
        def _():
            dz[...] = jnp.zeros_like(dz)

        dmid = jnp.zeros((rows, lanes), F32)
        for c in range(chunks):
            down = down_ref[:, c * down_rows : (c + 1) * down_rows, :].reshape(lanes, lanes)
            dmid += lax.dot_general(
                g_ref[:, c * lanes : (c + 1) * lanes], down, NT, preferred_element_type=F32
            )
        dgate = (dmid * a_ref[...]).astype(BF16)
        dup = (dmid * b_ref[...]).astype(BF16)
        dz[...] += lax.dot_general(
            dgate, gate_ref[...].reshape(model, lanes), NT, preferred_element_type=F32
        ) + lax.dot_general(dup, up_ref[...].reshape(model, lanes), NT, preferred_element_type=F32)

        @pl.when(step == pl.num_programs(0) - 1)
        def _():
            xhat, inverse = normalize(x_ref[...])
            e = dz[...] * gain_ref[...]
            inner = (
                e
                - jnp.mean(e, axis=1, keepdims=True)
                - xhat * jnp.mean(e * xhat, axis=1, keepdims=True)
            )
            out_ref[...] = (g_ref[...].astype(F32) + inverse * inner).astype(BF16)

    return pl.pallas_call(
        kernel,
        grid=(steps,),
        in_specs=[
            whole((rows, model)),
            pl.BlockSpec((rows, lanes), lambda j: (0, j)),
            pl.BlockSpec((rows, lanes), lambda j: (0, j)),
            whole((rows, model)),
            whole((1, model)),
            pl.BlockSpec((devices, shard_rows, lanes), lambda j: (0, j, 0)),
            pl.BlockSpec((devices, shard_rows, lanes), lambda j: (0, steps + j, 0)),
            pl.BlockSpec((holders, chunks * down_rows, lanes), lambda j: (j, 2, 0)),
        ],
        out_specs=whole((rows, model)),
        out_shape=SHAPE((rows, model), BF16),
        scratch_shapes=[pltpu.VMEM((rows, model), F32)],
        compiler_params=params(),
        cost_estimate=cost(6 * rows * model * hidden, 6 * model * hidden),
        name="block_backward",
    )(grad, gate_factor, up_factor, block_in, gain, packed, packed, packed)


def dp_pairs(move):
    pairs = []
    for z in range(4):
        for x in range(4):
            for core in range(2):
                tz, tx, tc = move(z, x, core)
                pairs.append(((z * 4 + x) * 2 + core, (tz * 4 + tx) * 2 + tc))
    return pairs


def sum_over_dp(value):
    value = value + lax.ppermute(value, "dp", dp_pairs(lambda z, x, c: (z, x, 1 - c)))
    for axis in ("x", "z"):
        parts = [value]
        for k in (1, 3, 2):
            move = (lambda z, x, c: (z, (x + k) % 4, c)) if axis == "x" else (lambda z, x, c: ((z + k) % 4, x, c))
            parts.append(lax.ppermute(value, "dp", dp_pairs(move)))
        if axis == "x":
            value = (parts[0] + parts[1]) + (parts[2] + parts[3])
    return parts


def parts_over_section(value):
    return [value] + [
        lax.ppermute(value, "section", [(i, (i + k) % 4) for i in range(4)]) for k in (1, 3, 2)
    ]


def parts_to_last_section(value):
    return [value] + [lax.ppermute(value, "section", [(i, 3)]) for i in (2, 0, 1)]


def per_device(
    teacher_logits, prototypes, head_weight, student_out, block_inputs, ln_gain, w_gate, w_up, w_down
):
    packed = lax.all_gather(pack_weights(w_gate[0], w_up[0], w_down[0], 512), "dp", axis=0)
    hidden = w_gate.shape[2]
    shard_rows, down_rows = w_gate.shape[1], w_down.shape[1]

    student, unit, radius = student_products(student_out, head_weight, prototypes)
    student_parts = parts_to_last_section(student)

    row_parts = []
    for _ in range(N_ITER - 1):
        column_parts = sum_over_dp(column_sums(teacher_logits, row_parts))
        row_parts = parts_over_section(row_sums(teacher_logits, column_parts))
    column_parts = sum_over_dp(column_sums(teacher_logits, row_parts))
    target_parts = parts_to_last_section(target_products(teacher_logits, column_parts, prototypes))

    block_in = block_inputs[0]
    gate_factor, up_factor = block_forward(block_in, ln_gain, packed, shard_rows, hidden)
    incoming = head_gradient(student_parts, target_parts, unit, radius, head_weight)

    section = lax.axis_index("section")
    result = None
    for turn in (3, 2, 1, 0):
        computed = block_backward(
            incoming, gate_factor, up_factor, block_in, ln_gain, packed, shard_rows, down_rows
        )
        result = computed if result is None else jnp.where(section == turn, computed, result)
        if turn:
            incoming = lax.ppermute(computed, "section", [(turn, turn - 1)])
    return result[None]


def solution(mesh):
    in_specs = (
        P("dp", "section"),
        P("section", None),
        P(),
        P("dp", None),
        P("section", "dp", None),
        P("section", None),
        P("section", "dp", None),
        P("section", "dp", None),
        P("section", "dp", None),
    )
    out_specs = P("section", "dp", None)
    return jax.shard_map(per_device, mesh=mesh, in_specs=in_specs, out_specs=out_specs, check_vma=False)
```

```python
import math

import jax
import jax.numpy as jnp
from jax import lax
from jax.experimental import pallas as pl
from jax.experimental.pallas import tpu as pltpu
from jax.sharding import PartitionSpec as P

TEACHER_SCALE = 1.0 / 0.07
STUDENT_SCALE = 1.0 / 0.1
EPS = 1e-06
N_ITER = 3
F32 = jnp.float32
BF16 = jnp.bfloat16
NT = (((1,), (1,)), ((), ()))
LOG2E = math.log2(math.e)
VMEM_LIMIT = 16 * 1024 * 1024
SHAPE = jax.ShapeDtypeStruct


def params(limit=VMEM_LIMIT):
    return pltpu.CompilerParams(vmem_limit_bytes=limit)


def cost(flops, size, transcendentals=0):
    return pl.CostEstimate(flops=flops, bytes_accessed=size, transcendentals=transcendentals)


def in_vmem():
    return pl.BlockSpec(memory_space=pltpu.VMEM)


def row_to_column(row):
    n = row.shape[1]
    eye = lax.broadcasted_iota(jnp.int32, (n, n), 0) == lax.broadcasted_iota(jnp.int32, (n, n), 1)
    return jnp.sum(jnp.where(eye, row, 0.0), axis=1, keepdims=True)


def column_to_row(column):
    n = column.shape[0]
    eye = lax.broadcasted_iota(jnp.int32, (n, n), 0) == lax.broadcasted_iota(jnp.int32, (n, n), 1)
    return jnp.sum(jnp.where(eye, column, 0.0), axis=0, keepdims=True)


def teacher_weights(logits):
    return jnp.exp2(logits.astype(F32) * (TEACHER_SCALE * LOG2E))


def add_all(refs):
    values = [ref[...] for ref in refs]
    while len(values) > 1:
        values = [a + b for a, b in zip(values[::2], values[1::2])] + values[len(values) & ~1 :]
    return values[0]


def lane_sums(value):
    parts = [value[:, k : k + 128] for k in range(0, value.shape[1], 128)]
    while len(parts) > 1:
        parts = [a + b for a, b in zip(parts[::2], parts[1::2])] + parts[len(parts) & ~1 :]
    return parts[0]


def column_sums(logits, row_parts, width=2048):
    rows, columns = logits.shape

    def kernel(l_ref, *refs):
        out_ref = refs[-1]
        if len(refs) > 1:
            scale = row_to_column(1.0 / add_all(refs[:-1]))
        for k in range(0, columns, width):
            weights = teacher_weights(l_ref[:, k : k + width])
            if len(refs) > 1:
                weights = weights * scale
            out_ref[:, k : k + width] = jnp.sum(weights, axis=0, keepdims=True)

    return pl.pallas_call(
        kernel,
        in_specs=[in_vmem()] * (1 + len(row_parts)),
        out_specs=in_vmem(),
        out_shape=SHAPE((1, columns), F32),
        compiler_params=params(),
        cost_estimate=cost(4 * rows * columns, 2 * rows * columns, rows * columns),
        name="column_sums",
    )(logits, *row_parts)


def row_sums(logits, column_parts, width=2048):
    rows, columns = logits.shape

    def kernel(l_ref, *refs):
        out_ref = refs[-1]
        total = jnp.zeros((rows, 128), F32)
        for k in range(0, columns, width):
            scale = 1.0 / add_all([ref.at[:, k : k + width] for ref in refs[:-1]])
            total += lane_sums(teacher_weights(l_ref[:, k : k + width]) * scale)
        out_ref[...] = column_to_row(jnp.sum(total, axis=1, keepdims=True))

    return pl.pallas_call(
        kernel,
        in_specs=[in_vmem()] * (1 + len(column_parts)),
        out_specs=in_vmem(),
        out_shape=SHAPE((1, rows), F32),
        compiler_params=params(),
        cost_estimate=cost(4 * rows * columns, 2 * rows * columns, rows * columns),
        name="row_sums",
    )(logits, *column_parts)


def target_products(logits, column_parts, prototypes, width=2048):
    rows, columns = logits.shape
    bottleneck = prototypes.shape[1]

    def kernel(l_ref, p_ref, *refs):
        out_ref = refs[-1]
        total = jnp.zeros((rows, 128), F32)
        acc = jnp.zeros((rows, bottleneck), F32)
        for k in range(0, columns, width):
            scale = 1.0 / add_all([ref.at[:, k : k + width] for ref in refs[:-1]])
            scaled = teacher_weights(l_ref[:, k : k + width]) * scale
            total += lane_sums(scaled)
            acc += jnp.dot(scaled.astype(BF16), p_ref[k : k + width, :], preferred_element_type=F32)
        out_ref[:rows, :] = acc
        sums = column_to_row(jnp.sum(total, axis=1, keepdims=True))
        out_ref[rows:, :] = jnp.broadcast_to(jnp.concatenate([sums, sums], axis=1), (8, bottleneck))

    return pl.pallas_call(
        kernel,
        in_specs=[in_vmem()] * (2 + len(column_parts)),
        out_specs=in_vmem(),
        out_shape=SHAPE((rows + 8, bottleneck), F32),
        compiler_params=params(),
        cost_estimate=cost(2 * rows * columns * bottleneck, 12 * 1024 * 1024, rows * columns),
        name="target_products",
    )(logits, prototypes, *column_parts)


def student_unit(student_out, head):
    rows, model = student_out.shape
    bottleneck = head.shape[1]

    def kernel(s_ref, h_ref, unit_ref, radius_ref):
        feature = jnp.dot(s_ref[...], h_ref[...], preferred_element_type=F32)
        radius = jnp.sqrt(jnp.sum(feature * feature, axis=1, keepdims=True) + EPS)
        unit_ref[...] = feature / radius
        radius_ref[...] = jnp.broadcast_to(radius, radius_ref.shape)

    return pl.pallas_call(
        kernel,
        in_specs=[in_vmem()] * 2,
        out_specs=[in_vmem()] * 2,
        out_shape=[SHAPE((rows, bottleneck), F32), SHAPE((rows, 128), F32)],
        compiler_params=params(),
        cost_estimate=cost(2 * rows * model * bottleneck, 2 * 1024 * 1024),
        name="student_unit",
    )(student_out, head)


def student_products(unit, prototypes, before, part, parts, width=2048):
    rows, bottleneck = unit.shape
    columns = prototypes.shape[0]
    span = columns // parts

    def kernel(u_ref, p_ref, *refs):
        out_ref = refs[-1]
        unit_b = u_ref[...].astype(BF16)
        total = jnp.zeros((rows, 128), F32)
        acc = jnp.zeros((rows, bottleneck), F32)
        for k in range(part * span, (part + 1) * span, width):
            block = p_ref[k : k + width, :]
            scores = lax.dot_general(unit_b, block, NT, preferred_element_type=F32)
            expo = jnp.exp2(scores * (STUDENT_SCALE * LOG2E))
            total += lane_sums(expo)
            acc += jnp.dot(expo.astype(BF16), block, preferred_element_type=F32)
        sums = column_to_row(jnp.sum(total, axis=1, keepdims=True))
        sums = jnp.broadcast_to(jnp.concatenate([sums, sums], axis=1), (8, bottleneck))
        if before is not None:
            acc += refs[0][:rows, :]
            sums += refs[0][rows:, :]
        out_ref[:rows, :] = acc
        out_ref[rows:, :] = sums

    extra = [] if before is None else [before]
    return pl.pallas_call(
        kernel,
        in_specs=[in_vmem()] * (2 + len(extra)),
        out_specs=in_vmem(),
        out_shape=SHAPE((rows + 8, bottleneck), F32),
        compiler_params=params(),
        cost_estimate=cost(4 * rows * span * bottleneck, 512 * span, rows * span),
        name="student_products",
    )(unit, prototypes, *extra)


def head_gradient(student_parts, target_parts, unit, radius, head):
    rows, bottleneck = unit.shape
    model = head.shape[0]
    count = len(student_parts)

    def kernel(*refs):
        unit_ref, radius_ref, h_ref, out_ref = refs[2 * count :]
        student = add_all(refs[:count])
        target = add_all(refs[count : 2 * count])
        dunit = (
            student[:rows, :] / row_to_column(student[rows : rows + 1, :rows])
            - target[:rows, :] / row_to_column(target[rows : rows + 1, :rows])
        ) * STUDENT_SCALE
        unit = unit_ref[...]
        along = jnp.sum(unit * dunit, axis=1, keepdims=True)
        dfeature = ((dunit - unit * along) / radius_ref[:, :1]).astype(BF16)
        out_ref[...] = lax.dot_general(h_ref[...], dfeature, NT, preferred_element_type=F32).astype(BF16)

    parts = list(student_parts) + list(target_parts)
    return pl.pallas_call(
        kernel,
        in_specs=[in_vmem()] * (2 * count + 3),
        out_specs=in_vmem(),
        out_shape=SHAPE((model, rows), BF16),
        compiler_params=params(),
        cost_estimate=cost(2 * rows * model * bottleneck, 3 * 1024 * 1024),
        name="head_gradient",
    )(*parts, unit, radius, head)


def pack_weights(w_gate, w_up, w_down, lanes):
    arrays = (w_gate, w_up, w_down)

    def kernel(*refs):
        out_ref = refs[-1]
        row = 0
        for ref in refs[:-1]:
            for k in range(0, ref.shape[1], lanes):
                out_ref[row : row + ref.shape[0], :] = ref[:, k : k + lanes]
                row += ref.shape[0]

    total = sum(w.shape[0] * w.shape[1] for w in arrays)
    return pl.pallas_call(
        kernel,
        in_specs=[in_vmem()] * 3,
        out_specs=in_vmem(),
        out_shape=SHAPE((total // lanes, lanes), BF16),
        compiler_params=params(),
        cost_estimate=cost(0, 4 * total),
        name="pack_weights",
    )(*arrays)


def block_forward(block_in, gain, packed, shard_rows, hidden):
    rows, model = block_in.shape
    devices, height, lanes = packed.shape
    steps = hidden // lanes

    def kernel(x_ref, gain_ref, w_ref, held, a_ref, b_ref, xhat_ref, inverse_ref, gain_out, sems):
        def copy(k):
            if k < 2 * steps:
                part = pl.ds(k * shard_rows, shard_rows)
            else:
                part = pl.ds(2 * steps * shard_rows, height - 2 * steps * shard_rows)
            return pltpu.make_async_copy(w_ref.at[:, part, :], held.at[:, part, :], sems.at[k])

        order = [k for j in range(steps) for k in (j, steps + j)] + [2 * steps]
        for k in order:
            copy(k).start()
        xfloat = x_ref[...].astype(F32)
        centered = xfloat - jnp.mean(xfloat, axis=1, keepdims=True)
        inverse = lax.rsqrt(jnp.mean(centered * centered, axis=1, keepdims=True) + EPS)
        xhat = centered * inverse
        z = (xhat * gain_ref[...]).astype(BF16)
        xhat_ref[...] = xhat.T
        inverse_ref[...] = column_to_row(inverse)
        gain_out[...] = jnp.broadcast_to(gain_ref[...], (rows, model)).T
        for j in range(steps):
            copy(j).wait()
            copy(steps + j).wait()
            gate_w = held[:, j * shard_rows : (j + 1) * shard_rows, :].reshape(model, lanes)
            up_w = held[:, (steps + j) * shard_rows : (steps + j + 1) * shard_rows, :].reshape(model, lanes)
            gate = jnp.dot(z, gate_w, preferred_element_type=F32)
            up = jnp.dot(z, up_w, preferred_element_type=F32)
            sigma = 1.0 / (1.0 + jnp.exp(-gate))
            a_ref[j * lanes : (j + 1) * lanes, :] = (up * sigma * (1.0 + gate * (1.0 - sigma))).T
            b_ref[j * lanes : (j + 1) * lanes, :] = (gate * sigma).T
        copy(2 * steps).wait()

    return pl.pallas_call(
        kernel,
        in_specs=[in_vmem(), in_vmem(), pl.BlockSpec(memory_space=pl.ANY)],
        out_specs=[in_vmem()] * 6,
        out_shape=[
            SHAPE(packed.shape, BF16),
            SHAPE((hidden, rows), F32),
            SHAPE((hidden, rows), F32),
            SHAPE((model, rows), F32),
            SHAPE((1, rows), F32),
            SHAPE((model, rows), F32),
        ],
        scratch_shapes=[pltpu.SemaphoreType.DMA((2 * steps + 1,))],
        compiler_params=params(),
        cost_estimate=cost(4 * rows * model * hidden, 12 * model * hidden, rows * hidden),
        name="block_forward",
    )(block_in, gain, packed)


def block_backward(grad, held, gate_factor, up_factor, xhat, inverse, gain, shard_rows, down_rows, height=384):
    model, rows = grad.shape
    hidden = gate_factor.shape[0]
    devices, _, lanes = held.shape
    steps = hidden // lanes
    chunks = model // lanes
    holders = lanes // down_rows
    down_start = 2 * steps * shard_rows

    def kernel(g_ref, w_ref, a_ref, b_ref, x_ref, inv_ref, gain_ref, out_ref, dgate, dup, scaled):
        for j in range(steps):
            span = slice(j * lanes, (j + 1) * lanes)
            dmid = jnp.zeros((lanes, rows), F32)
            for c in range(chunks):
                part = slice(down_start + c * down_rows, down_start + (c + 1) * down_rows)
                down = w_ref[j * holders : (j + 1) * holders, part, :].reshape(lanes, lanes)
                dmid += jnp.dot(down, g_ref[c * lanes : (c + 1) * lanes, :], preferred_element_type=F32)
            dgate[span, :] = (dmid * a_ref[span, :]).astype(BF16)
            dup[span, :] = (dmid * b_ref[span, :]).astype(BF16)
        sum_e = jnp.zeros((1, rows), F32)
        sum_ex = jnp.zeros((1, rows), F32)
        count = height // shard_rows
        for n in range(0, devices, count):
            dz = jnp.zeros((height, rows), F32)
            for j in range(steps):
                span = slice(j * lanes, (j + 1) * lanes)
                for factor, start in ((dgate, j), (dup, steps + j)):
                    part = slice(start * shard_rows, (start + 1) * shard_rows)
                    weights = w_ref[n : n + count, part, :].reshape(height, lanes)
                    dz += jnp.dot(weights, factor[span, :], preferred_element_type=F32)
            place = slice(n * shard_rows, n * shard_rows + height)
            e = dz * gain_ref[place, :]
            scaled[place, :] = e
            sum_e += jnp.sum(e, axis=0, keepdims=True)
            sum_ex += jnp.sum(e * x_ref[place, :], axis=0, keepdims=True)
        inner = scaled[...] - sum_e / model - x_ref[...] * (sum_ex / model)
        out_ref[...] = (g_ref[...].astype(F32) + inv_ref[...] * inner).astype(BF16)

    return pl.pallas_call(
        kernel,
        in_specs=[in_vmem()] * 7,
        out_specs=in_vmem(),
        out_shape=SHAPE((model, rows), BF16),
        scratch_shapes=[
            pltpu.VMEM((hidden, rows), BF16),
            pltpu.VMEM((hidden, rows), BF16),
            pltpu.VMEM((model, rows), F32),
        ],
        compiler_params=params(),
        cost_estimate=cost(6 * rows * model * hidden, 6 * model * hidden),
        name="block_backward",
    )(grad, held, gate_factor, up_factor, xhat, inverse, gain)


def dp_pairs(axis, flip):
    shift = {"core": 1, "x": 2, "z": 8}[axis]
    return [(i, i ^ (flip * shift)) for i in range(32)]


def after(value, *others):
    return lax.optimization_barrier((value, *others))[0]


def sum_over_dp(value, meanwhile=None):
    extra = None
    for step, (axis, flip) in enumerate((("core", 1), ("x", 1), ("x", 3), ("z", 1), ("z", 3))):
        other = lax.ppermute(value, "dp", dp_pairs(axis, flip))
        if axis == "z" and flip == 3:
            return [value, other], extra
        if step == 1 and meanwhile is not None:
            extra = meanwhile(value)
            other = after(other, *jax.tree.leaves(extra))
        value = value + other


def parts_over_section(value):
    value = value + lax.ppermute(value, "section", [(i, i ^ 1) for i in range(4)])
    return [value, lax.ppermute(value, "section", [(i, i ^ 3) for i in range(4)])]


def parts_to_last_section(value):
    return [value] + [lax.ppermute(value, "section", [(i, 3)]) for i in (2, 0, 1)]


def per_device(
    teacher_logits, prototypes, head_weight, student_out, block_inputs, ln_gain, w_gate, w_up, w_down
):
    packed = lax.all_gather(pack_weights(w_gate[0], w_up[0], w_down[0], 512), "dp", axis=0)
    hidden = w_gate.shape[2]
    shard_rows, down_rows = w_gate.shape[1], w_down.shape[1]

    def first_half(token):
        unit, radius = student_unit(after(student_out, token), head_weight)
        return unit, radius, student_products(unit, prototypes, None, 0, 2)

    column_parts, (unit, radius, student) = sum_over_dp(column_sums(teacher_logits, []), first_half)
    row_parts = parts_over_section(row_sums(teacher_logits, column_parts))
    column_parts, student = sum_over_dp(
        column_sums(teacher_logits, row_parts),
        lambda token: student_products(after(unit, token), prototypes, student, 1, 2),
    )
    row_parts = parts_over_section(row_sums(teacher_logits, column_parts))
    column_parts, student_parts = sum_over_dp(
        column_sums(teacher_logits, row_parts), lambda token: parts_to_last_section(after(student, token))
    )
    target = target_products(teacher_logits, column_parts, prototypes)
    target_parts = parts_to_last_section(target)

    held, *factors = block_forward(after(block_inputs[0], target), ln_gain, packed, shard_rows, hidden)
    incoming = head_gradient(student_parts, target_parts, unit, radius, head_weight)

    section = lax.axis_index("section")
    result = None
    for turn in (3, 2, 1, 0):
        computed = block_backward(incoming, held, *factors, shard_rows, down_rows)
        result = computed if result is None else jnp.where(section == turn, computed, result)
        if turn:
            incoming = lax.ppermute(computed, "section", [(turn, turn - 1)])
    return result.T[None]


def solution(mesh):
    in_specs = (
        P("dp", "section"),
        P("section", None),
        P(),
        P("dp", None),
        P("section", "dp", None),
        P("section", None),
        P("section", "dp", None),
        P("section", "dp", None),
        P("section", "dp", None),
    )
    out_specs = P("section", "dp", None)
    return jax.shard_map(per_device, mesh=mesh, in_specs=in_specs, out_specs=out_specs, check_vma=False)
```

```python
import math

import jax
import jax.numpy as jnp
from jax import lax
from jax.experimental import pallas as pl
from jax.experimental.pallas import tpu as pltpu
from jax.sharding import PartitionSpec as P

TEACHER_SCALE = 1.0 / 0.07
STUDENT_SCALE = 1.0 / 0.1
EPS = 1e-06
N_ITER = 3
F32 = jnp.float32
BF16 = jnp.bfloat16
NT = (((1,), (1,)), ((), ()))
LOG2E = math.log2(math.e)
VMEM_LIMIT = 16 * 1024 * 1024
LOGITS_LIMIT = 52 * 1024 * 1024
PROTOTYPES_LIMIT = 43 * 1024 * 1024
PACK_LIMIT = 63 * 1024 * 1024
SHAPE = jax.ShapeDtypeStruct


def params(limit=VMEM_LIMIT):
    return pltpu.CompilerParams(vmem_limit_bytes=limit)


def cost(flops, size, transcendentals=0):
    return pl.CostEstimate(flops=flops, bytes_accessed=size, transcendentals=transcendentals)


def in_hbm():
    return pl.BlockSpec(memory_space=pltpu.HBM)


def in_vmem():
    return pl.BlockSpec(memory_space=pltpu.VMEM)


def row_to_column(row):
    n = row.shape[1]
    eye = lax.broadcasted_iota(jnp.int32, (n, n), 0) == lax.broadcasted_iota(jnp.int32, (n, n), 1)
    return jnp.sum(jnp.where(eye, row, 0.0), axis=1, keepdims=True)


def column_to_row(column):
    n = column.shape[0]
    eye = lax.broadcasted_iota(jnp.int32, (n, n), 0) == lax.broadcasted_iota(jnp.int32, (n, n), 1)
    return jnp.sum(jnp.where(eye, column, 0.0), axis=0, keepdims=True)


def teacher_weights(logits):
    return jnp.exp2(logits.astype(F32) * (TEACHER_SCALE * LOG2E))


def add_all(refs):
    values = [ref[...].astype(F32) for ref in refs]
    while len(values) > 1:
        values = [a + b for a, b in zip(values[::2], values[1::2])] + values[len(values) & ~1 :]
    return values[0]


def lane_sums(value):
    parts = [value[:, k : k + 128] for k in range(0, value.shape[1], 128)]
    while len(parts) > 1:
        parts = [a + b for a, b in zip(parts[::2], parts[1::2])] + parts[len(parts) & ~1 :]
    return parts[0]


def column_sums(logits, row_parts, width=1024):
    rows, columns = logits.shape
    steps = columns // width
    first = not row_parts

    def kernel(l_ref, *refs):
        if first:
            out_ref, held, sems = refs
            copies = [
                pltpu.make_async_copy(
                    l_ref.at[:, pl.ds(k * width, width)], held.at[:, pl.ds(k * width, width)], sems.at[k]
                )
                for k in range(steps)
            ]
            for copy in copies:
                copy.start()
        else:
            out_ref, held = refs[-2], l_ref
            scale = row_to_column(1.0 / add_all(refs[:-2]))
        for k in range(steps):
            if first:
                copies[k].wait()
            weights = teacher_weights(held[:, k * width : (k + 1) * width])
            if not first:
                weights = weights * scale
            out_ref[k : k + 1, :] = jnp.sum(weights, axis=0, keepdims=True)

    return pl.pallas_call(
        kernel,
        in_specs=[in_hbm() if first else in_vmem()] + [in_vmem()] * len(row_parts),
        out_specs=[in_vmem()] * 2,
        out_shape=[SHAPE((steps, width), F32), SHAPE(logits.shape, BF16)],
        input_output_aliases={} if first else {0: 1},
        scratch_shapes=[pltpu.SemaphoreType.DMA((steps,))] if first else [],
        compiler_params=params(LOGITS_LIMIT if first else VMEM_LIMIT),
        cost_estimate=cost(4 * rows * columns, 2 * rows * columns, rows * columns),
        name="column_sums",
    )(logits, *row_parts)


def row_sums(logits, column_parts):
    rows, columns = logits.shape
    width = column_parts[0].shape[1]

    def kernel(l_ref, *refs):
        out_ref = refs[-2]
        scale = 1.0 / add_all(refs[:-2])
        total = jnp.zeros((rows, 128), F32)
        for k in range(columns // width):
            total += lane_sums(teacher_weights(l_ref[:, k * width : (k + 1) * width]) * scale[k : k + 1, :])
        out_ref[...] = column_to_row(jnp.sum(total, axis=1, keepdims=True))

    return pl.pallas_call(
        kernel,
        in_specs=[in_vmem()] * (1 + len(column_parts)),
        out_specs=[in_vmem()] * 2,
        out_shape=[SHAPE((1, rows), F32), SHAPE(logits.shape, BF16)],
        input_output_aliases={0: 1},
        compiler_params=params(),
        cost_estimate=cost(4 * rows * columns, 2 * rows * columns, rows * columns),
        name="row_sums",
    )(logits, *column_parts)


def target_products(logits, column_parts, prototypes):
    rows, columns = logits.shape
    width = column_parts[0].shape[1]
    bottleneck = prototypes.shape[1]

    def kernel(l_ref, p_ref, *refs):
        out_ref = refs[-1]
        scale = 1.0 / add_all(refs[:-1])
        total = jnp.zeros((rows, 128), F32)
        acc = jnp.zeros((rows, bottleneck), F32)
        for k in range(columns // width):
            span = slice(k * width, (k + 1) * width)
            scaled = teacher_weights(l_ref[:, span]) * scale[k : k + 1, :]
            total += lane_sums(scaled)
            acc += jnp.dot(scaled.astype(BF16), p_ref[span, :], preferred_element_type=F32)
        out_ref[:rows, :] = acc
        sums = column_to_row(jnp.sum(total, axis=1, keepdims=True))
        out_ref[rows:, :] = jnp.broadcast_to(jnp.concatenate([sums, sums], axis=1), (8, bottleneck))

    return pl.pallas_call(
        kernel,
        in_specs=[in_vmem()] * (2 + len(column_parts)),
        out_specs=in_vmem(),
        out_shape=SHAPE((rows + 8, bottleneck), F32),
        compiler_params=params(),
        cost_estimate=cost(2 * rows * columns * bottleneck, 12 * 1024 * 1024, rows * columns),
        name="target_products",
    )(logits, prototypes, *column_parts)


def student_unit(student_out, head):
    rows, model = student_out.shape
    bottleneck = head.shape[1]

    def kernel(s_ref, h_ref, unit_ref, radius_ref):
        feature = jnp.dot(s_ref[...], h_ref[...], preferred_element_type=F32)
        radius = jnp.sqrt(jnp.sum(feature * feature, axis=1, keepdims=True) + EPS)
        unit_ref[...] = feature / radius
        radius_ref[...] = jnp.broadcast_to(radius, radius_ref.shape)

    return pl.pallas_call(
        kernel,
        in_specs=[in_vmem()] * 2,
        out_specs=[in_vmem()] * 2,
        out_shape=[SHAPE((rows, bottleneck), F32), SHAPE((rows, 128), F32)],
        compiler_params=params(),
        cost_estimate=cost(2 * rows * model * bottleneck, 2 * 1024 * 1024),
        name="student_unit",
    )(student_out, head)


def student_products(unit, prototypes, before, part, parts, width=2048):
    rows, bottleneck = unit.shape
    columns = prototypes.shape[0]
    span = columns // parts
    first = before is None

    def kernel(u_ref, p_ref, *refs):
        if first:
            out_ref, held, sems = refs
            copies = [
                pltpu.make_async_copy(p_ref.at[pl.ds(k, width), :], held.at[pl.ds(k, width), :], sems.at[n])
                for n, k in enumerate(range(0, columns, width))
            ]
            for copy in copies:
                copy.start()
        else:
            before_ref, out_ref, _ = refs
            held = p_ref
        unit_b = u_ref[...].astype(BF16)
        total = jnp.zeros((rows, 128), F32)
        acc = jnp.zeros((rows, bottleneck), F32)
        for k in range(part * span, (part + 1) * span, width):
            if first:
                copies[k // width].wait()
            block = held[k : k + width, :]
            scores = lax.dot_general(unit_b, block, NT, preferred_element_type=F32)
            expo = jnp.exp2(scores * (STUDENT_SCALE * LOG2E))
            total += lane_sums(expo)
            acc += jnp.dot(expo.astype(BF16), block, preferred_element_type=F32)
        sums = column_to_row(jnp.sum(total, axis=1, keepdims=True))
        sums = jnp.broadcast_to(jnp.concatenate([sums, sums], axis=1), (8, bottleneck))
        if first:
            for copy in copies[span // width :]:
                copy.wait()
        else:
            acc += before_ref[:rows, :]
            sums += before_ref[rows:, :]
        out_ref[:rows, :] = acc
        out_ref[rows:, :] = sums

    return pl.pallas_call(
        kernel,
        in_specs=[in_vmem(), in_hbm() if first else in_vmem()]
        + ([] if first else [in_vmem()]),
        out_specs=[in_vmem()] * 2,
        out_shape=[SHAPE((rows + 8, bottleneck), F32), SHAPE(prototypes.shape, BF16)],
        input_output_aliases={} if first else {1: 1},
        scratch_shapes=[pltpu.SemaphoreType.DMA((columns // width,))] if first else [],
        compiler_params=params(PROTOTYPES_LIMIT if first else VMEM_LIMIT),
        cost_estimate=cost(4 * rows * span * bottleneck, 512 * span, rows * span),
        name="student_products",
    )(unit, prototypes, *([] if first else [before]))


def head_gradient(student_parts, target_parts, unit, radius, head):
    rows, bottleneck = unit.shape
    model = head.shape[0]
    count = len(student_parts)

    def kernel(*refs):
        unit_ref, radius_ref, h_ref, out_ref = refs[2 * count :]
        student = add_all(refs[:count])
        target = add_all(refs[count : 2 * count])
        dunit = (
            student[:rows, :] / row_to_column(student[rows : rows + 1, :rows])
            - target[:rows, :] / row_to_column(target[rows : rows + 1, :rows])
        ) * STUDENT_SCALE
        unit = unit_ref[...]
        along = jnp.sum(unit * dunit, axis=1, keepdims=True)
        dfeature = ((dunit - unit * along) / radius_ref[:, :1]).astype(BF16)
        out_ref[...] = lax.dot_general(h_ref[...], dfeature, NT, preferred_element_type=F32).astype(BF16)

    parts = list(student_parts) + list(target_parts)
    return pl.pallas_call(
        kernel,
        in_specs=[in_vmem()] * (2 * count + 3),
        out_specs=in_vmem(),
        out_shape=SHAPE((model, rows), BF16),
        compiler_params=params(),
        cost_estimate=cost(2 * rows * model * bottleneck, 3 * 1024 * 1024),
        name="head_gradient",
    )(*parts, unit, radius, head)


def pack_weights(w_gate, w_up, w_down, lanes):
    arrays = (w_gate, w_up, w_down)

    moves = []
    row = 0
    for index, w in enumerate(arrays):
        for k in range(0, w.shape[1], lanes):
            moves.append((index, k, row, w.shape[0]))
            row += w.shape[0]

    def kernel(*refs):
        out_ref, sems = refs[-2:]
        copies = [
            pltpu.make_async_copy(
                refs[index].at[:, pl.ds(k, lanes)], out_ref.at[pl.ds(row, height), :], sems.at[n]
            )
            for n, (index, k, row, height) in enumerate(moves)
        ]
        for copy in copies:
            copy.start()
        for copy in copies:
            copy.wait()

    total = sum(w.shape[0] * w.shape[1] for w in arrays)
    return pl.pallas_call(
        kernel,
        in_specs=[in_hbm()] * 3,
        out_specs=in_hbm(),
        out_shape=SHAPE((total // lanes, lanes), BF16),
        scratch_shapes=[pltpu.SemaphoreType.DMA((len(moves),))],
        compiler_params=params(PACK_LIMIT),
        cost_estimate=cost(0, 4 * total),
        name="pack_weights",
    )(*arrays)


def block_forward(block_in, gain, packed, shard_rows, hidden):
    rows, model = block_in.shape
    devices, height, lanes = packed.shape
    steps = hidden // lanes

    def kernel(x_ref, gain_ref, w_ref, held, a_ref, b_ref, xhat_ref, inverse_ref, gain_out, sems):
        def copy(k):
            if k < 2 * steps:
                part = pl.ds(k * shard_rows, shard_rows)
            else:
                part = pl.ds(2 * steps * shard_rows, height - 2 * steps * shard_rows)
            return pltpu.make_async_copy(w_ref.at[:, part, :], held.at[:, part, :], sems.at[k])

        order = [k for j in range(steps) for k in (j, steps + j)] + [2 * steps]
        for k in order:
            copy(k).start()
        xfloat = x_ref[...].astype(F32)
        centered = xfloat - jnp.mean(xfloat, axis=1, keepdims=True)
        inverse = lax.rsqrt(jnp.mean(centered * centered, axis=1, keepdims=True) + EPS)
        xhat = centered * inverse
        z = (xhat * gain_ref[...]).astype(BF16)
        xhat_ref[...] = xhat.T
        inverse_ref[...] = column_to_row(inverse)
        gain_out[...] = jnp.broadcast_to(gain_ref[...], (rows, model)).T
        for j in range(steps):
            copy(j).wait()
            copy(steps + j).wait()
            gate_w = held[:, j * shard_rows : (j + 1) * shard_rows, :].reshape(model, lanes)
            up_w = held[:, (steps + j) * shard_rows : (steps + j + 1) * shard_rows, :].reshape(model, lanes)
            gate = jnp.dot(z, gate_w, preferred_element_type=F32)
            up = jnp.dot(z, up_w, preferred_element_type=F32)
            sigma = 1.0 / (1.0 + jnp.exp(-gate))
            a_ref[j * lanes : (j + 1) * lanes, :] = (up * sigma * (1.0 + gate * (1.0 - sigma))).T
            b_ref[j * lanes : (j + 1) * lanes, :] = (gate * sigma).T
        copy(2 * steps).wait()

    return pl.pallas_call(
        kernel,
        in_specs=[in_vmem(), in_vmem(), in_hbm()],
        out_specs=[in_vmem()] * 6,
        out_shape=[
            SHAPE(packed.shape, BF16),
            SHAPE((hidden, rows), F32),
            SHAPE((hidden, rows), F32),
            SHAPE((model, rows), F32),
            SHAPE((1, rows), F32),
            SHAPE((model, rows), F32),
        ],
        scratch_shapes=[pltpu.SemaphoreType.DMA((2 * steps + 1,))],
        compiler_params=params(),
        cost_estimate=cost(4 * rows * model * hidden, 12 * model * hidden, rows * hidden),
        name="block_forward",
    )(block_in, gain, packed)


def block_backward(grad, state, shard_rows, down_rows, height=384):
    held, gate_factor = state[:2]
    model, rows = grad.shape
    hidden = gate_factor.shape[0]
    devices, _, lanes = held.shape
    steps = hidden // lanes
    chunks = model // lanes
    holders = lanes // down_rows
    down_start = 2 * steps * shard_rows

    def kernel(g_ref, w_ref, a_ref, b_ref, x_ref, inv_ref, gain_ref, out_ref, *refs):
        dgate, dup, scaled = refs[-3:]
        for j in range(steps):
            span = slice(j * lanes, (j + 1) * lanes)
            dmid = jnp.zeros((lanes, rows), F32)
            for c in range(chunks):
                part = slice(down_start + c * down_rows, down_start + (c + 1) * down_rows)
                down = w_ref[j * holders : (j + 1) * holders, part, :].reshape(lanes, lanes)
                dmid += jnp.dot(down, g_ref[c * lanes : (c + 1) * lanes, :], preferred_element_type=F32)
            dgate[span, :] = (dmid * a_ref[span, :]).astype(BF16)
            dup[span, :] = (dmid * b_ref[span, :]).astype(BF16)
        sum_e = jnp.zeros((1, rows), F32)
        sum_ex = jnp.zeros((1, rows), F32)
        count = height // shard_rows
        for n in range(0, devices, count):
            dz = jnp.zeros((height, rows), F32)
            for j in range(steps):
                span = slice(j * lanes, (j + 1) * lanes)
                for factor, start in ((dgate, j), (dup, steps + j)):
                    part = slice(start * shard_rows, (start + 1) * shard_rows)
                    weights = w_ref[n : n + count, part, :].reshape(height, lanes)
                    dz += jnp.dot(weights, factor[span, :], preferred_element_type=F32)
            place = slice(n * shard_rows, n * shard_rows + height)
            e = dz * gain_ref[place, :]
            scaled[place, :] = e
            sum_e += jnp.sum(e, axis=0, keepdims=True)
            sum_ex += jnp.sum(e * x_ref[place, :], axis=0, keepdims=True)
        inner = scaled[...] - sum_e / model - x_ref[...] * (sum_ex / model)
        out_ref[...] = (g_ref[...].astype(F32) + inv_ref[...] * inner).astype(BF16)

    return pl.pallas_call(
        kernel,
        in_specs=[in_vmem()] * 7,
        out_specs=[in_vmem()] * 7,
        out_shape=[SHAPE((model, rows), BF16)] + [SHAPE(a.shape, a.dtype) for a in state],
        input_output_aliases={i: i for i in range(1, 7)},
        scratch_shapes=[
            pltpu.VMEM((hidden, rows), BF16),
            pltpu.VMEM((hidden, rows), BF16),
            pltpu.VMEM((model, rows), F32),
        ],
        compiler_params=params(),
        cost_estimate=cost(6 * rows * model * hidden, 6 * model * hidden),
        name="block_backward",
    )(grad, *state)


def after(value, *others):
    return lax.optimization_barrier((value, *others))[0]


def dp_pairs(move):
    pairs = []
    for i in range(32):
        z, x, core = move(i // 8, i // 2 % 4, i % 2)
        pairs.append((i, (z % 4 * 4 + x % 4) * 2 + core))
    return pairs


STAGES = (
    [lambda z, x, c, k=k: (z, x + k, c) for k in (1, 3, 2)],
    [lambda z, x, c, k=k: (z + k, x, c) for k in (1, 3, 2)],
)


def sum_over_dp(value, meanwhile=(None, None)):
    value = value + lax.ppermute(value, "dp", dp_pairs(lambda z, x, c: (z, x, 1 - c)))
    parts = None
    for moves, work in zip(STAGES, meanwhile):
        if parts is not None:
            value = (parts[0] + parts[1].astype(F32)) + (parts[2].astype(F32) + parts[3].astype(F32))
        small = value.astype(BF16)
        parts = [value] + [lax.ppermute(small, "dp", dp_pairs(move)) for move in moves]
        if work is not None:
            parts[3] = after(parts[3], work(small))
    return parts


def parts_over_section(value):
    return [value] + [
        lax.ppermute(value, "section", [(i, (i + k) % 4) for i in range(4)]) for k in (1, 3, 2)
    ]


def parts_to_last_section(value):
    return [value] + [lax.ppermute(value, "section", [(i, 3)]) for i in (2, 0, 1)]


def per_device(
    teacher_logits, prototypes, head_weight, student_out, block_inputs, ln_gain, w_gate, w_up, w_down
):
    packed = lax.all_gather(pack_weights(w_gate[0], w_up[0], w_down[0], 512), "dp", axis=0)
    hidden = w_gate.shape[2]
    shard_rows, down_rows = w_gate.shape[1], w_down.shape[1]

    logits = teacher_logits
    made = {}

    def make_unit(token):
        made["unit"], made["radius"] = student_unit(after(student_out, token), head_weight)
        return made["unit"]

    def first_half(token):
        made["student"], made["p"] = student_products(after(made["unit"], token), prototypes, None, 0, 2)
        return made["student"]

    def second_half(token):
        made["student"], made["p"] = student_products(
            after(made["unit"], token), made["p"], made["student"], 1, 2
        )
        return made["student"]

    sums, logits = column_sums(logits, [])
    column_parts = sum_over_dp(sums, (make_unit, first_half))
    sums, logits = row_sums(logits, column_parts)
    sums, logits = column_sums(logits, parts_over_section(sums))
    column_parts = sum_over_dp(sums, (second_half, None))
    sums, logits = row_sums(logits, column_parts)
    sums, logits = column_sums(logits, parts_over_section(sums))
    student_parts = parts_to_last_section(after(made["student"], sums))
    column_parts = sum_over_dp(sums)
    target = target_products(logits, column_parts, made["p"])
    target_parts = parts_to_last_section(target)

    state = block_forward(after(block_inputs[0], target), ln_gain, packed, shard_rows, hidden)
    unit = after(made["unit"], state[4])
    incoming = head_gradient(student_parts, target_parts, unit, made["radius"], head_weight)

    section = lax.axis_index("section")
    result = None
    for turn in (3, 2, 1, 0):
        computed, *state = block_backward(incoming, state, shard_rows, down_rows)
        result = computed if result is None else jnp.where(section == turn, computed, result)
        if turn:
            incoming = lax.ppermute(computed, "section", [(turn, turn - 1)])
    return result.T[None]


def solution(mesh):
    in_specs = (
        P("dp", "section"),
        P("section", None),
        P(),
        P("dp", None),
        P("section", "dp", None),
        P("section", None),
        P("section", "dp", None),
        P("section", "dp", None),
        P("section", "dp", None),
    )
    out_specs = P("section", "dp", None)
    return jax.shard_map(per_device, mesh=mesh, in_specs=in_specs, out_specs=out_specs, check_vma=False)
```

```python
import math

import jax
import jax.numpy as jnp
from jax import lax
from jax.experimental import pallas as pl
from jax.experimental.pallas import tpu as pltpu
from jax.sharding import PartitionSpec as P

TEACHER_SCALE = 1.0 / 0.07
STUDENT_SCALE = 1.0 / 0.1
EPS = 1e-06
N_ITER = 3
F32 = jnp.float32
BF16 = jnp.bfloat16
NT = (((1,), (1,)), ((), ()))
LOG2E = math.log2(math.e)
VMEM_LIMIT = 16 * 1024 * 1024
LOGITS_LIMIT = 48 * 1024 * 1024
PROTOTYPES_LIMIT = 43 * 1024 * 1024
PACK_LIMIT = 55 * 1024 * 1024
SHAPE = jax.ShapeDtypeStruct


def params(limit=VMEM_LIMIT):
    return pltpu.CompilerParams(vmem_limit_bytes=limit)


def cost(flops, size, transcendentals=0):
    return pl.CostEstimate(flops=flops, bytes_accessed=size, transcendentals=transcendentals)


def in_hbm():
    return pl.BlockSpec(memory_space=pltpu.HBM)


def in_vmem():
    return pl.BlockSpec(memory_space=pltpu.VMEM)


def row_to_column(row):
    n = row.shape[1]
    eye = lax.broadcasted_iota(jnp.int32, (n, n), 0) == lax.broadcasted_iota(jnp.int32, (n, n), 1)
    return jnp.sum(jnp.where(eye, row, 0.0), axis=1, keepdims=True)


def column_to_row(column):
    n = column.shape[0]
    eye = lax.broadcasted_iota(jnp.int32, (n, n), 0) == lax.broadcasted_iota(jnp.int32, (n, n), 1)
    return jnp.sum(jnp.where(eye, column, 0.0), axis=0, keepdims=True)


def teacher_weights(logits):
    return jnp.exp2(logits.astype(F32) * (TEACHER_SCALE * LOG2E))


def add_all(refs):
    values = [ref[...].astype(F32) for ref in refs]
    while len(values) > 1:
        values = [a + b for a, b in zip(values[::2], values[1::2])] + values[len(values) & ~1 :]
    return values[0]


def lane_sums(value):
    parts = [value[:, k : k + 128] for k in range(0, value.shape[1], 128)]
    while len(parts) > 1:
        parts = [a + b for a, b in zip(parts[::2], parts[1::2])] + parts[len(parts) & ~1 :]
    return parts[0]


def column_sums(logits, row_parts, width=1024):
    rows, columns = logits.shape
    steps = columns // width
    first = not row_parts

    def kernel(l_ref, *refs):
        if first:
            out_ref, held, sems = refs
            copies = [
                pltpu.make_async_copy(
                    l_ref.at[:, pl.ds(k * width, width)], held.at[:, pl.ds(k * width, width)], sems.at[k]
                )
                for k in range(steps)
            ]
            for copy in copies:
                copy.start()
        else:
            out_ref, held = refs[-2], l_ref
            scale = row_to_column(1.0 / add_all(refs[:-2]))
        for k in range(steps):
            if first:
                copies[k].wait()
            weights = teacher_weights(held[:, k * width : (k + 1) * width])
            if not first:
                weights = weights * scale
            out_ref[k : k + 1, :] = jnp.sum(weights, axis=0, keepdims=True)

    return pl.pallas_call(
        kernel,
        in_specs=[in_hbm() if first else in_vmem()] + [in_vmem()] * len(row_parts),
        out_specs=[in_vmem()] * 2,
        out_shape=[SHAPE((steps, width), F32), SHAPE(logits.shape, BF16)],
        input_output_aliases={} if first else {0: 1},
        scratch_shapes=[pltpu.SemaphoreType.DMA((steps,))] if first else [],
        compiler_params=params(LOGITS_LIMIT if first else VMEM_LIMIT),
        cost_estimate=cost(4 * rows * columns, 2 * rows * columns, rows * columns),
        name="column_sums",
    )(logits, *row_parts)


def row_sums(logits, column_parts):
    rows, columns = logits.shape
    width = column_parts[0].shape[1]

    def kernel(l_ref, *refs):
        out_ref = refs[-2]
        scale = 1.0 / add_all(refs[:-2])
        total = jnp.zeros((rows, 128), F32)
        for k in range(columns // width):
            total += lane_sums(teacher_weights(l_ref[:, k * width : (k + 1) * width]) * scale[k : k + 1, :])
        out_ref[...] = column_to_row(jnp.sum(total, axis=1, keepdims=True))

    return pl.pallas_call(
        kernel,
        in_specs=[in_vmem()] * (1 + len(column_parts)),
        out_specs=[in_vmem()] * 2,
        out_shape=[SHAPE((1, rows), F32), SHAPE(logits.shape, BF16)],
        input_output_aliases={0: 1},
        compiler_params=params(),
        cost_estimate=cost(4 * rows * columns, 2 * rows * columns, rows * columns),
        name="row_sums",
    )(logits, *column_parts)


def target_products(logits, column_parts, prototypes):
    rows, columns = logits.shape
    width = column_parts[0].shape[1]
    bottleneck = prototypes.shape[1]

    def kernel(l_ref, p_ref, *refs):
        out_ref = refs[-1]
        scale = 1.0 / add_all(refs[:-1])
        total = jnp.zeros((rows, 128), F32)
        acc = jnp.zeros((rows, bottleneck), F32)
        for k in range(columns // width):
            span = slice(k * width, (k + 1) * width)
            scaled = teacher_weights(l_ref[:, span]) * scale[k : k + 1, :]
            total += lane_sums(scaled)
            acc += jnp.dot(scaled.astype(BF16), p_ref[span, :], preferred_element_type=F32)
        out_ref[:rows, :] = acc
        sums = column_to_row(jnp.sum(total, axis=1, keepdims=True))
        out_ref[rows:, :] = jnp.broadcast_to(jnp.concatenate([sums, sums], axis=1), (8, bottleneck))

    return pl.pallas_call(
        kernel,
        in_specs=[in_vmem()] * (2 + len(column_parts)),
        out_specs=in_vmem(),
        out_shape=SHAPE((rows + 8, bottleneck), F32),
        compiler_params=params(),
        cost_estimate=cost(2 * rows * columns * bottleneck, 12 * 1024 * 1024, rows * columns),
        name="target_products",
    )(logits, prototypes, *column_parts)


def student_unit(student_out, head):
    rows, model = student_out.shape
    bottleneck = head.shape[1]

    def kernel(s_ref, h_ref, unit_ref, radius_ref):
        feature = jnp.dot(s_ref[...], h_ref[...], preferred_element_type=F32)
        radius = jnp.sqrt(jnp.sum(feature * feature, axis=1, keepdims=True) + EPS)
        unit_ref[...] = feature / radius
        radius_ref[...] = jnp.broadcast_to(radius, radius_ref.shape)

    return pl.pallas_call(
        kernel,
        in_specs=[in_vmem()] * 2,
        out_specs=[in_vmem()] * 2,
        out_shape=[SHAPE((rows, bottleneck), F32), SHAPE((rows, 128), F32)],
        compiler_params=params(),
        cost_estimate=cost(2 * rows * model * bottleneck, 2 * 1024 * 1024),
        name="student_unit",
    )(student_out, head)


def student_products(unit, prototypes, before, part, parts, width=2048):
    rows, bottleneck = unit.shape
    columns = prototypes.shape[0]
    span = columns // parts
    first = before is None

    def kernel(u_ref, p_ref, *refs):
        if first:
            out_ref, held, sems = refs
            copies = [
                pltpu.make_async_copy(p_ref.at[pl.ds(k, width), :], held.at[pl.ds(k, width), :], sems.at[n])
                for n, k in enumerate(range(0, columns, width))
            ]
            for copy in copies:
                copy.start()
        else:
            before_ref, out_ref, _ = refs
            held = p_ref
        unit_b = u_ref[...].astype(BF16)
        total = jnp.zeros((rows, 128), F32)
        acc = jnp.zeros((rows, bottleneck), F32)
        for k in range(part * span, (part + 1) * span, width):
            if first:
                copies[k // width].wait()
            block = held[k : k + width, :]
            scores = lax.dot_general(unit_b, block, NT, preferred_element_type=F32)
            expo = jnp.exp2(scores * (STUDENT_SCALE * LOG2E))
            total += lane_sums(expo)
            acc += jnp.dot(expo.astype(BF16), block, preferred_element_type=F32)
        sums = column_to_row(jnp.sum(total, axis=1, keepdims=True))
        sums = jnp.broadcast_to(jnp.concatenate([sums, sums], axis=1), (8, bottleneck))
        if first:
            for copy in copies[span // width :]:
                copy.wait()
        else:
            acc += before_ref[:rows, :]
            sums += before_ref[rows:, :]
        out_ref[:rows, :] = acc
        out_ref[rows:, :] = sums

    return pl.pallas_call(
        kernel,
        in_specs=[in_vmem(), in_hbm() if first else in_vmem()]
        + ([] if first else [in_vmem()]),
        out_specs=[in_vmem()] * 2,
        out_shape=[SHAPE((rows + 8, bottleneck), F32), SHAPE(prototypes.shape, BF16)],
        input_output_aliases={} if first else {1: 1},
        scratch_shapes=[pltpu.SemaphoreType.DMA((columns // width,))] if first else [],
        compiler_params=params(PROTOTYPES_LIMIT if first else VMEM_LIMIT),
        cost_estimate=cost(4 * rows * span * bottleneck, 512 * span, rows * span),
        name="student_products",
    )(unit, prototypes, *([] if first else [before]))


def head_gradient(student_parts, target_parts, unit, radius, head):
    rows, bottleneck = unit.shape
    model = head.shape[0]
    count, total = len(student_parts), len(student_parts) + len(target_parts)

    def kernel(*refs):
        unit_ref, radius_ref, h_ref, out_ref = refs[total:]
        student = add_all(refs[:count])
        target = add_all(refs[count:total])
        dunit = (
            student[:rows, :] / row_to_column(student[rows : rows + 1, :rows])
            - target[:rows, :] / row_to_column(target[rows : rows + 1, :rows])
        ) * STUDENT_SCALE
        unit = unit_ref[...]
        along = jnp.sum(unit * dunit, axis=1, keepdims=True)
        dfeature = ((dunit - unit * along) / radius_ref[:, :1]).astype(BF16)
        out_ref[...] = lax.dot_general(h_ref[...], dfeature, NT, preferred_element_type=F32).astype(BF16)

    parts = list(student_parts) + list(target_parts)
    return pl.pallas_call(
        kernel,
        in_specs=[in_vmem()] * (total + 3),
        out_specs=in_vmem(),
        out_shape=SHAPE((model, rows), BF16),
        compiler_params=params(),
        cost_estimate=cost(2 * rows * model * bottleneck, 3 * 1024 * 1024),
        name="head_gradient",
    )(*parts, unit, radius, head)


def pack_weights(w_gate, w_up, w_down, lanes):
    arrays = (w_gate, w_up, w_down)

    moves = []
    row = 0
    for index, w in enumerate(arrays):
        for k in range(0, w.shape[1], lanes):
            moves.append((index, k, row, w.shape[0]))
            row += w.shape[0]

    def kernel(*refs):
        out_ref, sems = refs[-2:]
        copies = [
            pltpu.make_async_copy(
                refs[index].at[:, pl.ds(k, lanes)], out_ref.at[pl.ds(row, height), :], sems.at[n]
            )
            for n, (index, k, row, height) in enumerate(moves)
        ]
        for copy in copies:
            copy.start()
        for copy in copies:
            copy.wait()

    total = sum(w.shape[0] * w.shape[1] for w in arrays)
    return pl.pallas_call(
        kernel,
        in_specs=[in_hbm()] * 3,
        out_specs=in_vmem(),
        out_shape=SHAPE((total // lanes, lanes), BF16),
        scratch_shapes=[pltpu.SemaphoreType.DMA((len(moves),))],
        compiler_params=params(PACK_LIMIT),
        cost_estimate=cost(0, 4 * total),
        name="pack_weights",
    )(*arrays)


def block_forward(block_in, gain, packed, shard_rows, hidden):
    rows, model = block_in.shape
    devices, height, lanes = packed.shape
    steps = hidden // lanes

    def kernel(x_ref, gain_ref, w_ref, held, a_ref, b_ref, xhat_ref, inverse_ref, gain_out, sems):
        def copy(k):
            if k < 2 * steps:
                part = pl.ds(k * shard_rows, shard_rows)
            else:
                part = pl.ds(2 * steps * shard_rows, height - 2 * steps * shard_rows)
            return pltpu.make_async_copy(w_ref.at[:, part, :], held.at[:, part, :], sems.at[k])

        order = [k for j in range(steps) for k in (j, steps + j)] + [2 * steps]
        for k in order:
            copy(k).start()
        xfloat = x_ref[...].astype(F32)
        centered = xfloat - jnp.mean(xfloat, axis=1, keepdims=True)
        inverse = lax.rsqrt(jnp.mean(centered * centered, axis=1, keepdims=True) + EPS)
        xhat = centered * inverse
        z = (xhat * gain_ref[...]).astype(BF16)
        xhat_ref[...] = xhat.T
        inverse_ref[...] = column_to_row(inverse)
        gain_out[...] = jnp.broadcast_to(gain_ref[...], (rows, model)).T
        for j in range(steps):
            copy(j).wait()
            copy(steps + j).wait()
            gate_w = held[:, j * shard_rows : (j + 1) * shard_rows, :].reshape(model, lanes)
            up_w = held[:, (steps + j) * shard_rows : (steps + j + 1) * shard_rows, :].reshape(model, lanes)
            gate = jnp.dot(z, gate_w, preferred_element_type=F32)
            up = jnp.dot(z, up_w, preferred_element_type=F32)
            sigma = 1.0 / (1.0 + jnp.exp(-gate))
            a_ref[j * lanes : (j + 1) * lanes, :] = (up * sigma * (1.0 + gate * (1.0 - sigma))).T
            b_ref[j * lanes : (j + 1) * lanes, :] = (gate * sigma).T
        copy(2 * steps).wait()

    return pl.pallas_call(
        kernel,
        in_specs=[in_vmem(), in_vmem(), in_hbm()],
        out_specs=[in_vmem()] * 6,
        out_shape=[
            SHAPE(packed.shape, BF16),
            SHAPE((hidden, rows), F32),
            SHAPE((hidden, rows), F32),
            SHAPE((model, rows), F32),
            SHAPE((1, rows), F32),
            SHAPE((model, rows), F32),
        ],
        scratch_shapes=[pltpu.SemaphoreType.DMA((2 * steps + 1,))],
        compiler_params=params(),
        cost_estimate=cost(4 * rows * model * hidden, 12 * model * hidden, rows * hidden),
        name="block_forward",
    )(block_in, gain, packed)


def block_backward(grad, state, earlier, shard_rows, down_rows, height=384):
    held, gate_factor = state[:2]
    model, rows = grad.shape
    hidden = gate_factor.shape[0]
    devices, _, lanes = held.shape
    steps = hidden // lanes
    chunks = model // lanes
    holders = lanes // down_rows
    down_start = 2 * steps * shard_rows
    final = bool(earlier)

    def kernel(g_ref, w_ref, a_ref, b_ref, x_ref, inv_ref, gain_ref, *refs):
        earlier_refs, out_ref = refs[: len(earlier)], refs[len(earlier)]
        dgate, dup, scaled = refs[-3:]
        for j in range(steps):
            span = slice(j * lanes, (j + 1) * lanes)
            dmid = jnp.zeros((lanes, rows), F32)
            for c in range(chunks):
                part = slice(down_start + c * down_rows, down_start + (c + 1) * down_rows)
                down = w_ref[j * holders : (j + 1) * holders, part, :].reshape(lanes, lanes)
                dmid += jnp.dot(down, g_ref[c * lanes : (c + 1) * lanes, :], preferred_element_type=F32)
            dgate[span, :] = (dmid * a_ref[span, :]).astype(BF16)
            dup[span, :] = (dmid * b_ref[span, :]).astype(BF16)
        sum_e = jnp.zeros((1, rows), F32)
        sum_ex = jnp.zeros((1, rows), F32)
        count = height // shard_rows
        for n in range(0, devices, count):
            dz = jnp.zeros((height, rows), F32)
            for j in range(steps):
                span = slice(j * lanes, (j + 1) * lanes)
                for factor, start in ((dgate, j), (dup, steps + j)):
                    part = slice(start * shard_rows, (start + 1) * shard_rows)
                    weights = w_ref[n : n + count, part, :].reshape(height, lanes)
                    dz += jnp.dot(weights, factor[span, :], preferred_element_type=F32)
            place = slice(n * shard_rows, n * shard_rows + height)
            e = dz * gain_ref[place, :]
            scaled[place, :] = e
            sum_e += jnp.sum(e, axis=0, keepdims=True)
            sum_ex += jnp.sum(e * x_ref[place, :], axis=0, keepdims=True)
        inner = scaled[...] - sum_e / model - x_ref[...] * (sum_ex / model)
        result = g_ref[...].astype(F32) + inv_ref[...] * inner
        if final:
            section = lax.axis_index("section")
            for turn, ref in enumerate(earlier_refs):
                result = jnp.where(section == len(earlier) - turn, ref[...].astype(F32), result)
            result = result.T
        out_ref[...] = result.astype(BF16)

    return pl.pallas_call(
        kernel,
        in_specs=[in_vmem()] * (7 + len(earlier)),
        out_specs=[in_vmem()] * (1 if final else 7),
        out_shape=[SHAPE((rows, model) if final else (model, rows), BF16)]
        + ([] if final else [SHAPE(a.shape, a.dtype) for a in state]),
        input_output_aliases={} if final else {i: i for i in range(1, 7)},
        scratch_shapes=[
            pltpu.VMEM((hidden, rows), BF16),
            pltpu.VMEM((hidden, rows), BF16),
            pltpu.VMEM((model, rows), F32),
        ],
        compiler_params=params(),
        cost_estimate=cost(6 * rows * model * hidden, 6 * model * hidden),
        name="block_backward",
    )(grad, *state, *earlier)


def after(value, *others):
    return lax.optimization_barrier((value, *others))[0]


def dp_pairs(move):
    pairs = []
    for i in range(32):
        z, x, core = move(i // 8, i // 2 % 4, i % 2)
        pairs.append((i, (z % 4 * 4 + x % 4) * 2 + core))
    return pairs


STAGES = (
    [lambda z, x, c, k=k: (z, x + k, c) for k in (1, 3, 2)],
    [lambda z, x, c, k=k: (z + k, x, c) for k in (1, 3, 2)],
)


def sum_over_dp(value, meanwhile=(None, None)):
    value = value + lax.ppermute(value, "dp", dp_pairs(lambda z, x, c: (z, x, 1 - c)))
    parts = None
    for moves, work in zip(STAGES, meanwhile):
        if parts is not None:
            value = (parts[0] + parts[1].astype(F32)) + (parts[2].astype(F32) + parts[3].astype(F32))
        small = value.astype(BF16)
        parts = [value] + [lax.ppermute(small, "dp", dp_pairs(move)) for move in moves]
        if work is not None:
            parts[3] = after(parts[3], work(small))
    return parts


def parts_over_section(value):
    return [value] + [
        lax.ppermute(value, "section", [(i, (i + k) % 4) for i in range(4)]) for k in (1, 3, 2)
    ]


def parts_to_last_section(value, core=None):
    if core is None:
        return [lax.ppermute(value, "section", [(i, 3)]) for i in (2, 0, 1)]
    return [
        lax.ppermute(value, ("dp", "section"), [(d * 4 + i, d * 4 + 3) for d in range(core, 32, 2)])
        for i in (2, 0, 1)
    ]


def per_device(
    teacher_logits, prototypes, head_weight, student_out, block_inputs, ln_gain, w_gate, w_up, w_down
):
    packed = lax.all_gather(pack_weights(w_gate[0], w_up[0], w_down[0], 512), "dp", axis=0)
    hidden = w_gate.shape[2]
    shard_rows, down_rows = w_gate.shape[1], w_down.shape[1]

    logits = teacher_logits
    made = {}

    def make_unit(token):
        made["unit"], made["radius"] = student_unit(after(student_out, token), head_weight)
        return made["unit"]

    def first_half(token):
        made["student"], made["p"] = student_products(after(made["unit"], token), prototypes, None, 0, 2)
        return made["student"]

    def second_half(token):
        made["student"], made["p"] = student_products(
            after(made["unit"], token), made["p"], made["student"], 1, 2
        )
        return made["student"]

    sums, logits = column_sums(logits, [])
    column_parts = sum_over_dp(sums, (make_unit, first_half))
    sums, logits = row_sums(logits, column_parts)
    sums, logits = column_sums(logits, parts_over_section(sums))
    column_parts = sum_over_dp(sums, (second_half, None))
    sums, logits = row_sums(logits, column_parts)
    sums, logits = column_sums(logits, parts_over_section(sums))
    student = after(made["student"], sums)
    student_parts = [student] + parts_to_last_section(student)
    column_parts = sum_over_dp(sums)
    target = target_products(logits, column_parts, made["p"])
    target_parts = [target] + parts_to_last_section(target, 0)

    state = block_forward(after(block_inputs[0], target), ln_gain, packed, shard_rows, hidden)
    target_parts += parts_to_last_section(after(target, state[4]), 1)
    unit = made["unit"]
    incoming = head_gradient(student_parts, target_parts, unit, made["radius"], head_weight)

    results = []
    for turn in (3, 2, 1):
        computed, *state = block_backward(incoming, state, (), shard_rows, down_rows)
        results.append(computed)
        incoming = lax.ppermute(computed, "section", [(turn, turn - 1)])
    return block_backward(incoming, state, results, shard_rows, down_rows)[0][None]


def solution(mesh):
    in_specs = (
        P("dp", "section"),
        P("section", None),
        P(),
        P("dp", None),
        P("section", "dp", None),
        P("section", None),
        P("section", "dp", None),
        P("section", "dp", None),
        P("section", "dp", None),
    )
    out_specs = P("section", "dp", None)
    return jax.shard_map(per_device, mesh=mesh, in_specs=in_specs, out_specs=out_specs, check_vma=False)
```

```python
import math

import jax
import jax.numpy as jnp
from jax import lax
from jax.experimental import pallas as pl
from jax.experimental.pallas import tpu as pltpu
from jax.sharding import PartitionSpec as P

TEACHER_SCALE = 1.0 / 0.07
STUDENT_SCALE = 1.0 / 0.1
EPS = 1e-06
N_ITER = 3
F32 = jnp.float32
BF16 = jnp.bfloat16
NT = (((1,), (1,)), ((), ()))
LOG2E = math.log2(math.e)
VMEM_LIMIT = 16 * 1024 * 1024
LOGITS_LIMIT = 48 * 1024 * 1024
PROTOTYPES_LIMIT = 43 * 1024 * 1024
PACK_LIMIT = 55 * 1024 * 1024
SHAPE = jax.ShapeDtypeStruct


def params(limit=VMEM_LIMIT):
    return pltpu.CompilerParams(vmem_limit_bytes=limit)


def cost(flops, size, transcendentals=0):
    return pl.CostEstimate(flops=flops, bytes_accessed=size, transcendentals=transcendentals)


def in_hbm():
    return pl.BlockSpec(memory_space=pltpu.HBM)


def in_vmem():
    return pl.BlockSpec(memory_space=pltpu.VMEM)


def row_to_column(row):
    n = row.shape[1]
    eye = lax.broadcasted_iota(jnp.int32, (n, n), 0) == lax.broadcasted_iota(jnp.int32, (n, n), 1)
    return jnp.sum(jnp.where(eye, row, 0.0), axis=1, keepdims=True)


def column_to_row(column):
    n = column.shape[0]
    eye = lax.broadcasted_iota(jnp.int32, (n, n), 0) == lax.broadcasted_iota(jnp.int32, (n, n), 1)
    return jnp.sum(jnp.where(eye, column, 0.0), axis=0, keepdims=True)


def teacher_weights(logits):
    return jnp.exp2(logits.astype(F32) * (TEACHER_SCALE * LOG2E))


def add_all(refs):
    values = [ref[...].astype(F32) for ref in refs]
    while len(values) > 1:
        values = [a + b for a, b in zip(values[::2], values[1::2])] + values[len(values) & ~1 :]
    return values[0]


def lane_sums(value):
    parts = [value[:, k : k + 128] for k in range(0, value.shape[1], 128)]
    while len(parts) > 1:
        parts = [a + b for a, b in zip(parts[::2], parts[1::2])] + parts[len(parts) & ~1 :]
    return parts[0]


def column_sums(logits, row_parts, width=1024):
    rows, columns = logits.shape
    steps = columns // width
    first = not row_parts

    def kernel(l_ref, *refs):
        if first:
            out_ref, held, sems = refs
            copies = [
                pltpu.make_async_copy(
                    l_ref.at[:, pl.ds(k * width, width)], held.at[:, pl.ds(k * width, width)], sems.at[k]
                )
                for k in range(steps)
            ]
            for copy in copies:
                copy.start()
        else:
            out_ref, held = refs[-2], l_ref
            scale = row_to_column(1.0 / add_all(refs[:-2]))
        for k in range(steps):
            if first:
                copies[k].wait()
            weights = teacher_weights(held[:, k * width : (k + 1) * width])
            if not first:
                weights = weights * scale
            out_ref[k : k + 1, :] = jnp.sum(weights, axis=0, keepdims=True)

    return pl.pallas_call(
        kernel,
        in_specs=[in_hbm() if first else in_vmem()] + [in_vmem()] * len(row_parts),
        out_specs=[in_vmem()] * 2,
        out_shape=[SHAPE((steps, width), F32), SHAPE(logits.shape, BF16)],
        input_output_aliases={} if first else {0: 1},
        scratch_shapes=[pltpu.SemaphoreType.DMA((steps,))] if first else [],
        compiler_params=params(LOGITS_LIMIT if first else VMEM_LIMIT),
        cost_estimate=cost(4 * rows * columns, 2 * rows * columns, rows * columns),
        name="column_sums",
    )(logits, *row_parts)


def row_sums(logits, column_parts):
    rows, columns = logits.shape
    width = column_parts[0].shape[1]

    def kernel(l_ref, *refs):
        out_ref = refs[-2]
        scale = 1.0 / add_all(refs[:-2])
        total = jnp.zeros((rows, 128), F32)
        for k in range(columns // width):
            total += lane_sums(teacher_weights(l_ref[:, k * width : (k + 1) * width]) * scale[k : k + 1, :])
        out_ref[...] = column_to_row(jnp.sum(total, axis=1, keepdims=True))

    return pl.pallas_call(
        kernel,
        in_specs=[in_vmem()] * (1 + len(column_parts)),
        out_specs=[in_vmem()] * 2,
        out_shape=[SHAPE((1, rows), F32), SHAPE(logits.shape, BF16)],
        input_output_aliases={0: 1},
        compiler_params=params(),
        cost_estimate=cost(4 * rows * columns, 2 * rows * columns, rows * columns),
        name="row_sums",
    )(logits, *column_parts)


def target_products(logits, column_parts, prototypes):
    rows, columns = logits.shape
    width = column_parts[0].shape[1]
    bottleneck = prototypes.shape[1]

    def kernel(l_ref, p_ref, *refs):
        out_ref = refs[-1]
        scale = 1.0 / add_all(refs[:-1])
        total = jnp.zeros((rows, 128), F32)
        acc = jnp.zeros((rows, bottleneck), F32)
        for k in range(columns // width):
            span = slice(k * width, (k + 1) * width)
            scaled = teacher_weights(l_ref[:, span]) * scale[k : k + 1, :]
            total += lane_sums(scaled)
            acc += jnp.dot(scaled.astype(BF16), p_ref[span, :], preferred_element_type=F32)
        out_ref[:rows, :] = acc
        sums = column_to_row(jnp.sum(total, axis=1, keepdims=True))
        out_ref[rows:, :] = jnp.broadcast_to(jnp.concatenate([sums, sums], axis=1), (8, bottleneck))

    return pl.pallas_call(
        kernel,
        in_specs=[in_vmem()] * (2 + len(column_parts)),
        out_specs=in_vmem(),
        out_shape=SHAPE((rows + 8, bottleneck), F32),
        compiler_params=params(),
        cost_estimate=cost(2 * rows * columns * bottleneck, 12 * 1024 * 1024, rows * columns),
        name="target_products",
    )(logits, prototypes, *column_parts)


def student_unit(student_out, head):
    rows, model = student_out.shape
    bottleneck = head.shape[1]

    def kernel(s_ref, h_ref, unit_ref, radius_ref):
        feature = jnp.dot(s_ref[...], h_ref[...], preferred_element_type=F32)
        radius = jnp.sqrt(jnp.sum(feature * feature, axis=1, keepdims=True) + EPS)
        unit_ref[...] = feature / radius
        radius_ref[...] = jnp.broadcast_to(radius, radius_ref.shape)

    return pl.pallas_call(
        kernel,
        in_specs=[in_vmem()] * 2,
        out_specs=[in_vmem()] * 2,
        out_shape=[SHAPE((rows, bottleneck), F32), SHAPE((rows, 128), F32)],
        compiler_params=params(),
        cost_estimate=cost(2 * rows * model * bottleneck, 2 * 1024 * 1024),
        name="student_unit",
    )(student_out, head)


def student_products(unit, prototypes, before, part, parts, width=2048):
    rows, bottleneck = unit.shape
    columns = prototypes.shape[0]
    span = columns // parts
    first = before is None

    def kernel(u_ref, p_ref, *refs):
        if first:
            out_ref, held, sems = refs
            copies = [
                pltpu.make_async_copy(p_ref.at[pl.ds(k, width), :], held.at[pl.ds(k, width), :], sems.at[n])
                for n, k in enumerate(range(0, columns, width))
            ]
            for copy in copies:
                copy.start()
        else:
            before_ref, out_ref, _ = refs
            held = p_ref
        unit_b = u_ref[...].astype(BF16)
        total = jnp.zeros((rows, 128), F32)
        acc = jnp.zeros((rows, bottleneck), F32)
        for k in range(part * span, (part + 1) * span, width):
            if first:
                copies[k // width].wait()
            block = held[k : k + width, :]
            scores = lax.dot_general(unit_b, block, NT, preferred_element_type=F32)
            expo = jnp.exp2(scores * (STUDENT_SCALE * LOG2E))
            total += lane_sums(expo)
            acc += jnp.dot(expo.astype(BF16), block, preferred_element_type=F32)
        sums = column_to_row(jnp.sum(total, axis=1, keepdims=True))
        sums = jnp.broadcast_to(jnp.concatenate([sums, sums], axis=1), (8, bottleneck))
        if first:
            for copy in copies[span // width :]:
                copy.wait()
        else:
            acc += before_ref[:rows, :]
            sums += before_ref[rows:, :]
        out_ref[:rows, :] = acc
        out_ref[rows:, :] = sums

    return pl.pallas_call(
        kernel,
        in_specs=[in_vmem(), in_hbm() if first else in_vmem()]
        + ([] if first else [in_vmem()]),
        out_specs=[in_vmem()] * 2,
        out_shape=[SHAPE((rows + 8, bottleneck), F32), SHAPE(prototypes.shape, BF16)],
        input_output_aliases={} if first else {1: 1},
        scratch_shapes=[pltpu.SemaphoreType.DMA((columns // width,))] if first else [],
        compiler_params=params(PROTOTYPES_LIMIT if first else VMEM_LIMIT),
        cost_estimate=cost(4 * rows * span * bottleneck, 512 * span, rows * span),
        name="student_products",
    )(unit, prototypes, *([] if first else [before]))


def head_gradient(student_parts, target_parts, unit, radius, head):
    rows, bottleneck = unit.shape
    model = head.shape[0]
    count, total = len(student_parts), len(student_parts) + len(target_parts)

    def kernel(*refs):
        unit_ref, radius_ref, h_ref, out_ref = refs[total:]
        student = add_all(refs[:count])
        target = add_all(refs[count:total])
        dunit = (
            student[:rows, :] / row_to_column(student[rows : rows + 1, :rows])
            - target[:rows, :] / row_to_column(target[rows : rows + 1, :rows])
        ) * STUDENT_SCALE
        unit = unit_ref[...]
        along = jnp.sum(unit * dunit, axis=1, keepdims=True)
        dfeature = ((dunit - unit * along) / radius_ref[:, :1]).astype(BF16)
        out_ref[...] = lax.dot_general(h_ref[...], dfeature, NT, preferred_element_type=F32).astype(BF16)

    parts = list(student_parts) + list(target_parts)
    return pl.pallas_call(
        kernel,
        in_specs=[in_vmem()] * (total + 3),
        out_specs=in_vmem(),
        out_shape=SHAPE((model, rows), BF16),
        compiler_params=params(),
        cost_estimate=cost(2 * rows * model * bottleneck, 3 * 1024 * 1024),
        name="head_gradient",
    )(*parts, unit, radius, head)


def pack_weights(w_gate, w_up, w_down, lanes):
    arrays = (w_gate, w_up, w_down)

    moves = []
    row = 0
    for index, w in enumerate(arrays):
        for k in range(0, w.shape[1], lanes):
            moves.append((index, k, row, w.shape[0]))
            row += w.shape[0]

    def kernel(*refs):
        out_ref, sems = refs[-2:]
        copies = [
            pltpu.make_async_copy(
                refs[index].at[:, pl.ds(k, lanes)], out_ref.at[pl.ds(row, height), :], sems.at[n]
            )
            for n, (index, k, row, height) in enumerate(moves)
        ]
        for copy in copies:
            copy.start()
        for copy in copies:
            copy.wait()

    total = sum(w.shape[0] * w.shape[1] for w in arrays)
    return pl.pallas_call(
        kernel,
        in_specs=[in_hbm()] * 3,
        out_specs=in_vmem(),
        out_shape=SHAPE((total // lanes, lanes), BF16),
        scratch_shapes=[pltpu.SemaphoreType.DMA((len(moves),))],
        compiler_params=params(PACK_LIMIT),
        cost_estimate=cost(0, 4 * total),
        name="pack_weights",
    )(*arrays)


def block_forward(block_in, gain, packed, shard_rows, hidden):
    rows, model = block_in.shape
    devices, height, lanes = packed.shape
    steps = hidden // lanes

    def kernel(x_ref, gain_ref, w_ref, held, a_ref, b_ref, xhat_ref, inverse_ref, gain_out, sems):
        def copy(k):
            if k < 2 * steps:
                part = pl.ds(k * shard_rows, shard_rows)
            else:
                part = pl.ds(2 * steps * shard_rows, height - 2 * steps * shard_rows)
            return pltpu.make_async_copy(w_ref.at[:, part, :], held.at[:, part, :], sems.at[k])

        order = [k for j in range(steps) for k in (j, steps + j)] + [2 * steps]
        for k in order:
            copy(k).start()
        xfloat = x_ref[...].astype(F32)
        centered = xfloat - jnp.mean(xfloat, axis=1, keepdims=True)
        inverse = lax.rsqrt(jnp.mean(centered * centered, axis=1, keepdims=True) + EPS)
        xhat = centered * inverse
        z = (xhat * gain_ref[...]).astype(BF16)
        xhat_ref[...] = xhat.T
        inverse_ref[...] = column_to_row(inverse)
        gain_out[...] = jnp.broadcast_to(gain_ref[...], (rows, model)).T
        for j in range(steps):
            copy(j).wait()
            copy(steps + j).wait()
            gate_w = held[:, j * shard_rows : (j + 1) * shard_rows, :].reshape(model, lanes)
            up_w = held[:, (steps + j) * shard_rows : (steps + j + 1) * shard_rows, :].reshape(model, lanes)
            gate = jnp.dot(z, gate_w, preferred_element_type=F32)
            up = jnp.dot(z, up_w, preferred_element_type=F32)
            sigma = 1.0 / (1.0 + jnp.exp(-gate))
            a_ref[j * lanes : (j + 1) * lanes, :] = (up * sigma * (1.0 + gate * (1.0 - sigma))).T
            b_ref[j * lanes : (j + 1) * lanes, :] = (gate * sigma).T
        copy(2 * steps).wait()

    return pl.pallas_call(
        kernel,
        in_specs=[in_vmem(), in_vmem(), in_hbm()],
        out_specs=[in_vmem()] * 6,
        out_shape=[
            SHAPE(packed.shape, BF16),
            SHAPE((hidden, rows), F32),
            SHAPE((hidden, rows), F32),
            SHAPE((model, rows), F32),
            SHAPE((1, rows), F32),
            SHAPE((model, rows), F32),
        ],
        scratch_shapes=[pltpu.SemaphoreType.DMA((2 * steps + 1,))],
        compiler_params=params(),
        cost_estimate=cost(4 * rows * model * hidden, 12 * model * hidden, rows * hidden),
        name="block_forward",
    )(block_in, gain, packed)


def block_backward(grad, state, earlier, shard_rows, down_rows, height=384):
    held, gate_factor = state[:2]
    model, rows = grad.shape
    hidden = gate_factor.shape[0]
    devices, _, lanes = held.shape
    steps = hidden // lanes
    chunks = model // lanes
    holders = lanes // down_rows
    down_start = 2 * steps * shard_rows
    final = bool(earlier)

    def kernel(g_ref, w_ref, a_ref, b_ref, x_ref, inv_ref, gain_ref, *refs):
        earlier_refs, out_ref = refs[: len(earlier)], refs[len(earlier)]
        dgate, dup, scaled = refs[-3:]
        for j in range(steps):
            span = slice(j * lanes, (j + 1) * lanes)
            dmid = jnp.zeros((lanes, rows), F32)
            for c in range(chunks):
                part = slice(down_start + c * down_rows, down_start + (c + 1) * down_rows)
                down = w_ref[j * holders : (j + 1) * holders, part, :].reshape(lanes, lanes)
                dmid += jnp.dot(down, g_ref[c * lanes : (c + 1) * lanes, :], preferred_element_type=F32)
            dgate[span, :] = (dmid * a_ref[span, :]).astype(BF16)
            dup[span, :] = (dmid * b_ref[span, :]).astype(BF16)
        sum_e = jnp.zeros((1, rows), F32)
        sum_ex = jnp.zeros((1, rows), F32)
        count = height // shard_rows
        for n in range(0, devices, count):
            dz = jnp.zeros((height, rows), F32)
            for j in range(steps):
                span = slice(j * lanes, (j + 1) * lanes)
                for factor, start in ((dgate, j), (dup, steps + j)):
                    part = slice(start * shard_rows, (start + 1) * shard_rows)
                    weights = w_ref[n : n + count, part, :].reshape(height, lanes)
                    dz += jnp.dot(weights, factor[span, :], preferred_element_type=F32)
            place = slice(n * shard_rows, n * shard_rows + height)
            e = dz * gain_ref[place, :]
            scaled[place, :] = e
            sum_e += jnp.sum(e, axis=0, keepdims=True)
            sum_ex += jnp.sum(e * x_ref[place, :], axis=0, keepdims=True)
        inner = scaled[...] - sum_e / model - x_ref[...] * (sum_ex / model)
        result = g_ref[...].astype(F32) + inv_ref[...] * inner
        if final:
            section = lax.axis_index("section")
            for turn, ref in enumerate(earlier_refs):
                result = jnp.where(section == len(earlier) - turn, ref[...].astype(F32), result)
            result = result.T
        out_ref[...] = result.astype(BF16)

    return pl.pallas_call(
        kernel,
        in_specs=[in_vmem()] * (7 + len(earlier)),
        out_specs=[in_vmem()] * (1 if final else 7),
        out_shape=[SHAPE((rows, model) if final else (model, rows), BF16)]
        + ([] if final else [SHAPE(a.shape, a.dtype) for a in state]),
        input_output_aliases={} if final else {i: i for i in range(1, 7)},
        scratch_shapes=[
            pltpu.VMEM((hidden, rows), BF16),
            pltpu.VMEM((hidden, rows), BF16),
            pltpu.VMEM((model, rows), F32),
        ],
        compiler_params=params(),
        cost_estimate=cost(6 * rows * model * hidden, 6 * model * hidden),
        name="block_backward",
    )(grad, *state, *earlier)


def after(value, *others):
    return lax.optimization_barrier((value, *others))[0]


def dp_pairs(move):
    pairs = []
    for i in range(32):
        z, x, core = move(i // 8, i // 2 % 4, i % 2)
        pairs.append((i, (z % 4 * 4 + x % 4) * 2 + core))
    return pairs


STAGES = (
    [lambda z, x, c, k=k: (z, x + k, c) for k in (1, 3, 2)],
    [lambda z, x, c, k=k: (z + k, x, c) for k in (1, 3, 2)],
)


def sum_over_dp(value, meanwhile=(None, None)):
    value = value + lax.ppermute(value, "dp", dp_pairs(lambda z, x, c: (z, x, 1 - c)))
    parts = None
    for moves, work in zip(STAGES, meanwhile):
        if parts is not None:
            value = (parts[0] + parts[1].astype(F32)) + (parts[2].astype(F32) + parts[3].astype(F32))
        small = value.astype(BF16)
        parts = [value] + [lax.ppermute(small, "dp", dp_pairs(move)) for move in moves]
        if work is not None:
            parts[3] = after(parts[3], work(small))
    return parts


def parts_over_section(value):
    return [value] + [
        lax.ppermute(value, "section", [(i, (i + k) % 4) for i in range(4)]) for k in (1, 3, 2)
    ]


def parts_to_last_section(value, core):
    return [
        lax.ppermute(value, ("dp", "section"), [(d * 4 + i, d * 4 + 3) for d in range(core, 32, 2)])
        for i in (2, 0, 1)
    ]


def per_device(
    teacher_logits, prototypes, head_weight, student_out, block_inputs, ln_gain, w_gate, w_up, w_down
):
    packed = lax.all_gather(pack_weights(w_gate[0], w_up[0], w_down[0], 512), "dp", axis=0)
    hidden = w_gate.shape[2]
    shard_rows, down_rows = w_gate.shape[1], w_down.shape[1]

    logits = teacher_logits
    made = {}

    def make_unit(token):
        made["unit"], made["radius"] = student_unit(after(student_out, token), head_weight)
        return made["unit"]

    def first_half(token):
        made["student"], made["p"] = student_products(after(made["unit"], token), prototypes, None, 0, 2)
        return made["student"]

    def second_half(token):
        made["student"], made["p"] = student_products(
            after(made["unit"], token), made["p"], made["student"], 1, 2
        )
        return made["student"]

    def first_hop(token):
        student = after(made["student"], token)
        made["student"] = student + lax.ppermute(student, "section", [(1, 2), (0, 3)])
        return made["student"]

    def second_hop(token):
        student = after(made["student"], token)
        made["parts"] = [student, lax.ppermute(student, "section", [(2, 3)])]
        return made["parts"][1]

    sums, logits = column_sums(logits, [])
    column_parts = sum_over_dp(sums, (make_unit, first_half))
    sums, logits = row_sums(logits, column_parts)
    sums, logits = column_sums(logits, parts_over_section(sums))
    column_parts = sum_over_dp(sums, (second_half, first_hop))
    sums, logits = row_sums(logits, column_parts)
    sums, logits = column_sums(logits, parts_over_section(sums))
    column_parts = sum_over_dp(sums, (second_hop, None))
    target = target_products(logits, column_parts, made["p"])
    target_parts = [target] + parts_to_last_section(target, 0)

    state = block_forward(after(block_inputs[0], target), ln_gain, packed, shard_rows, hidden)
    target_parts += parts_to_last_section(after(target, state[4]), 1)
    unit = made["unit"]
    incoming = head_gradient(made["parts"], target_parts, unit, made["radius"], head_weight)

    results = []
    for turn in (3, 2, 1):
        computed, *state = block_backward(incoming, state, (), shard_rows, down_rows)
        results.append(computed)
        incoming = lax.ppermute(computed, "section", [(turn, turn - 1)])
    return block_backward(incoming, state, results, shard_rows, down_rows)[0][None]


def solution(mesh):
    in_specs = (
        P("dp", "section"),
        P("section", None),
        P(),
        P("dp", None),
        P("section", "dp", None),
        P("section", None),
        P("section", "dp", None),
        P("section", "dp", None),
        P("section", "dp", None),
    )
    out_specs = P("section", "dp", None)
    return jax.shard_map(per_device, mesh=mesh, in_specs=in_specs, out_specs=out_specs, check_vma=False)
```

```python
import math

import jax
import jax.numpy as jnp
from jax import lax
from jax.experimental import pallas as pl
from jax.experimental.pallas import tpu as pltpu
from jax.sharding import PartitionSpec as P

TEACHER_SCALE = 1.0 / 0.07
STUDENT_SCALE = 1.0 / 0.1
EPS = 1e-06
N_ITER = 3
F32 = jnp.float32
BF16 = jnp.bfloat16
NT = (((1,), (1,)), ((), ()))
LOG2E = math.log2(math.e)
VMEM_LIMIT = 16 * 1024 * 1024
LOGITS_LIMIT = 48 * 1024 * 1024
PROTOTYPES_LIMIT = 43 * 1024 * 1024
PACK_LIMIT = 55 * 1024 * 1024
SHAPE = jax.ShapeDtypeStruct


def params(limit=VMEM_LIMIT):
    return pltpu.CompilerParams(vmem_limit_bytes=limit)


def cost(flops, size, transcendentals=0):
    return pl.CostEstimate(flops=flops, bytes_accessed=size, transcendentals=transcendentals)


def in_hbm():
    return pl.BlockSpec(memory_space=pltpu.HBM)


def in_vmem():
    return pl.BlockSpec(memory_space=pltpu.VMEM)


def row_to_column(row):
    n = row.shape[1]
    eye = lax.broadcasted_iota(jnp.int32, (n, n), 0) == lax.broadcasted_iota(jnp.int32, (n, n), 1)
    return jnp.sum(jnp.where(eye, row, 0.0), axis=1, keepdims=True)


def column_to_row(column):
    n = column.shape[0]
    eye = lax.broadcasted_iota(jnp.int32, (n, n), 0) == lax.broadcasted_iota(jnp.int32, (n, n), 1)
    return jnp.sum(jnp.where(eye, column, 0.0), axis=0, keepdims=True)


def teacher_weights(logits):
    return jnp.exp2(logits.astype(F32) * (TEACHER_SCALE * LOG2E))


def add_all(refs):
    values = [ref[...].astype(F32) for ref in refs]
    while len(values) > 1:
        values = [a + b for a, b in zip(values[::2], values[1::2])] + values[len(values) & ~1 :]
    return values[0]


def lane_sums(value):
    parts = [value[:, k : k + 128] for k in range(0, value.shape[1], 128)]
    while len(parts) > 1:
        parts = [a + b for a, b in zip(parts[::2], parts[1::2])] + parts[len(parts) & ~1 :]
    return parts[0]


def column_sums(logits, row_parts, width=1024):
    rows, columns = logits.shape
    steps = columns // width
    first = not row_parts

    def kernel(l_ref, *refs):
        if first:
            out_ref, held, sems = refs
            copies = [
                pltpu.make_async_copy(
                    l_ref.at[:, pl.ds(k * width, width)], held.at[:, pl.ds(k * width, width)], sems.at[k]
                )
                for k in range(steps)
            ]
            for copy in copies:
                copy.start()
        else:
            out_ref, held = refs[-2], l_ref
            scale = row_to_column(1.0 / add_all(refs[:-2]))
        for k in range(steps):
            if first:
                copies[k].wait()
            weights = teacher_weights(held[:, k * width : (k + 1) * width])
            if not first:
                weights = weights * scale
            out_ref[k : k + 1, :] = jnp.sum(weights, axis=0, keepdims=True)

    return pl.pallas_call(
        kernel,
        in_specs=[in_hbm() if first else in_vmem()] + [in_vmem()] * len(row_parts),
        out_specs=[in_vmem()] * 2,
        out_shape=[SHAPE((steps, width), F32), SHAPE(logits.shape, BF16)],
        input_output_aliases={} if first else {0: 1},
        scratch_shapes=[pltpu.SemaphoreType.DMA((steps,))] if first else [],
        compiler_params=params(LOGITS_LIMIT if first else VMEM_LIMIT),
        cost_estimate=cost(4 * rows * columns, 2 * rows * columns, rows * columns),
        name="column_sums",
    )(logits, *row_parts)


def row_sums(logits, column_parts):
    rows, columns = logits.shape
    width = column_parts[0].shape[1]

    def kernel(l_ref, *refs):
        out_ref = refs[-2]
        scale = 1.0 / add_all(refs[:-2])
        total = jnp.zeros((rows, 128), F32)
        for k in range(columns // width):
            total += lane_sums(teacher_weights(l_ref[:, k * width : (k + 1) * width]) * scale[k : k + 1, :])
        out_ref[...] = column_to_row(jnp.sum(total, axis=1, keepdims=True))

    return pl.pallas_call(
        kernel,
        in_specs=[in_vmem()] * (1 + len(column_parts)),
        out_specs=[in_vmem()] * 2,
        out_shape=[SHAPE((1, rows), F32), SHAPE(logits.shape, BF16)],
        input_output_aliases={0: 1},
        compiler_params=params(),
        cost_estimate=cost(4 * rows * columns, 2 * rows * columns, rows * columns),
        name="row_sums",
    )(logits, *column_parts)


def target_products(logits, column_parts, prototypes):
    rows, columns = logits.shape
    width = column_parts[0].shape[1]
    bottleneck = prototypes.shape[1]

    def kernel(l_ref, p_ref, *refs):
        out_ref = refs[-1]
        scale = 1.0 / add_all(refs[:-1])
        total = jnp.zeros((rows, 128), F32)
        acc = jnp.zeros((rows, bottleneck), F32)
        for k in range(columns // width):
            span = slice(k * width, (k + 1) * width)
            scaled = teacher_weights(l_ref[:, span]) * scale[k : k + 1, :]
            total += lane_sums(scaled)
            acc += jnp.dot(scaled.astype(BF16), p_ref[span, :], preferred_element_type=F32)
        out_ref[:rows, :] = acc
        sums = column_to_row(jnp.sum(total, axis=1, keepdims=True))
        out_ref[rows:, :] = jnp.broadcast_to(jnp.concatenate([sums, sums], axis=1), (8, bottleneck))

    return pl.pallas_call(
        kernel,
        in_specs=[in_vmem()] * (2 + len(column_parts)),
        out_specs=in_vmem(),
        out_shape=SHAPE((rows + 8, bottleneck), F32),
        compiler_params=params(),
        cost_estimate=cost(2 * rows * columns * bottleneck, 12 * 1024 * 1024, rows * columns),
        name="target_products",
    )(logits, prototypes, *column_parts)


def student_unit(student_out, head):
    rows, model = student_out.shape
    bottleneck = head.shape[1]

    def kernel(s_ref, h_ref, unit_ref, radius_ref):
        feature = jnp.dot(s_ref[...], h_ref[...], preferred_element_type=F32)
        radius = jnp.sqrt(jnp.sum(feature * feature, axis=1, keepdims=True) + EPS)
        unit_ref[...] = feature / radius
        radius_ref[...] = jnp.broadcast_to(radius, radius_ref.shape)

    return pl.pallas_call(
        kernel,
        in_specs=[in_vmem()] * 2,
        out_specs=[in_vmem()] * 2,
        out_shape=[SHAPE((rows, bottleneck), F32), SHAPE((rows, 128), F32)],
        compiler_params=params(),
        cost_estimate=cost(2 * rows * model * bottleneck, 2 * 1024 * 1024),
        name="student_unit",
    )(student_out, head)


def student_products(unit, prototypes, before, part, parts, width=2048):
    rows, bottleneck = unit.shape
    columns = prototypes.shape[0]
    span = columns // parts
    first = before is None

    def kernel(u_ref, p_ref, *refs):
        if first:
            out_ref, held, sems = refs
            copies = [
                pltpu.make_async_copy(p_ref.at[pl.ds(k, width), :], held.at[pl.ds(k, width), :], sems.at[n])
                for n, k in enumerate(range(0, columns, width))
            ]
            for copy in copies:
                copy.start()
        else:
            before_ref, out_ref, _ = refs
            held = p_ref
        unit_b = u_ref[...].astype(BF16)
        total = jnp.zeros((rows, 128), F32)
        acc = jnp.zeros((rows, bottleneck), F32)
        for k in range(part * span, (part + 1) * span, width):
            if first:
                copies[k // width].wait()
            block = held[k : k + width, :]
            scores = lax.dot_general(unit_b, block, NT, preferred_element_type=F32)
            expo = jnp.exp2(scores * (STUDENT_SCALE * LOG2E))
            total += lane_sums(expo)
            acc += jnp.dot(expo.astype(BF16), block, preferred_element_type=F32)
        sums = column_to_row(jnp.sum(total, axis=1, keepdims=True))
        sums = jnp.broadcast_to(jnp.concatenate([sums, sums], axis=1), (8, bottleneck))
        if first:
            for copy in copies[span // width :]:
                copy.wait()
        else:
            acc += before_ref[:rows, :]
            sums += before_ref[rows:, :]
        out_ref[:rows, :] = acc
        out_ref[rows:, :] = sums

    return pl.pallas_call(
        kernel,
        in_specs=[in_vmem(), in_hbm() if first else in_vmem()]
        + ([] if first else [in_vmem()]),
        out_specs=[in_vmem()] * 2,
        out_shape=[SHAPE((rows + 8, bottleneck), F32), SHAPE(prototypes.shape, BF16)],
        input_output_aliases={} if first else {1: 1},
        scratch_shapes=[pltpu.SemaphoreType.DMA((columns // width,))] if first else [],
        compiler_params=params(PROTOTYPES_LIMIT if first else VMEM_LIMIT),
        cost_estimate=cost(4 * rows * span * bottleneck, 512 * span, rows * span),
        name="student_products",
    )(unit, prototypes, *([] if first else [before]))


def head_gradient(student_parts, target_parts, unit, radius, head):
    rows, bottleneck = unit.shape
    model = head.shape[0]
    count, total = len(student_parts), len(student_parts) + len(target_parts)

    def kernel(*refs):
        unit_ref, radius_ref, h_ref, out_ref = refs[total:]
        student = add_all(refs[:count])
        target = add_all(refs[count:total])
        dunit = (
            student[:rows, :] / row_to_column(student[rows : rows + 1, :rows])
            - target[:rows, :] / row_to_column(target[rows : rows + 1, :rows])
        ) * STUDENT_SCALE
        unit = unit_ref[...]
        along = jnp.sum(unit * dunit, axis=1, keepdims=True)
        dfeature = ((dunit - unit * along) / radius_ref[:, :1]).astype(BF16)
        out_ref[...] = lax.dot_general(h_ref[...], dfeature, NT, preferred_element_type=F32).astype(BF16)

    parts = list(student_parts) + list(target_parts)
    return pl.pallas_call(
        kernel,
        in_specs=[in_vmem()] * (total + 3),
        out_specs=in_vmem(),
        out_shape=SHAPE((model, rows), BF16),
        compiler_params=params(),
        cost_estimate=cost(2 * rows * model * bottleneck, 3 * 1024 * 1024),
        name="head_gradient",
    )(*parts, unit, radius, head)


def pack_weights(w_gate, w_up, w_down, lanes):
    arrays = (w_gate, w_up, w_down)

    moves = []
    row = 0
    for index, w in enumerate(arrays):
        for k in range(0, w.shape[1], lanes):
            moves.append((index, k, row, w.shape[0]))
            row += w.shape[0]

    def kernel(*refs):
        out_ref, sems = refs[-2:]
        copies = [
            pltpu.make_async_copy(
                refs[index].at[:, pl.ds(k, lanes)], out_ref.at[pl.ds(row, height), :], sems.at[n]
            )
            for n, (index, k, row, height) in enumerate(moves)
        ]
        for copy in copies:
            copy.start()
        for copy in copies:
            copy.wait()

    total = sum(w.shape[0] * w.shape[1] for w in arrays)
    return pl.pallas_call(
        kernel,
        in_specs=[in_hbm()] * 3,
        out_specs=in_vmem(),
        out_shape=SHAPE((total // lanes, lanes), BF16),
        scratch_shapes=[pltpu.SemaphoreType.DMA((len(moves),))],
        compiler_params=params(PACK_LIMIT),
        cost_estimate=cost(0, 4 * total),
        name="pack_weights",
    )(*arrays)


def block_forward(block_in, gain, packed, shard_rows, hidden):
    rows, model = block_in.shape
    devices, height, lanes = packed.shape
    steps = hidden // lanes

    def kernel(x_ref, gain_ref, w_ref, held, a_ref, b_ref, xhat_ref, inverse_ref, gain_out, sems):
        def copy(k):
            if k < 2 * steps:
                part = pl.ds(k * shard_rows, shard_rows)
            else:
                part = pl.ds(2 * steps * shard_rows, height - 2 * steps * shard_rows)
            return pltpu.make_async_copy(w_ref.at[:, part, :], held.at[:, part, :], sems.at[k])

        order = [k for j in range(steps) for k in (j, steps + j)] + [2 * steps]
        for k in order:
            copy(k).start()
        xfloat = x_ref[...].astype(F32)
        centered = xfloat - jnp.mean(xfloat, axis=1, keepdims=True)
        inverse = lax.rsqrt(jnp.mean(centered * centered, axis=1, keepdims=True) + EPS)
        xhat = centered * inverse
        z = (xhat * gain_ref[...]).astype(BF16)
        xhat_ref[...] = xhat.T
        inverse_ref[...] = column_to_row(inverse)
        gain_out[...] = jnp.broadcast_to(gain_ref[...], (rows, model)).T
        for j in range(steps):
            copy(j).wait()
            copy(steps + j).wait()
            gate_w = held[:, j * shard_rows : (j + 1) * shard_rows, :].reshape(model, lanes)
            up_w = held[:, (steps + j) * shard_rows : (steps + j + 1) * shard_rows, :].reshape(model, lanes)
            gate = jnp.dot(z, gate_w, preferred_element_type=F32)
            up = jnp.dot(z, up_w, preferred_element_type=F32)
            sigma = 1.0 / (1.0 + jnp.exp(-gate))
            a_ref[j * lanes : (j + 1) * lanes, :] = (up * sigma * (1.0 + gate * (1.0 - sigma))).T
            b_ref[j * lanes : (j + 1) * lanes, :] = (gate * sigma).T
        copy(2 * steps).wait()

    return pl.pallas_call(
        kernel,
        in_specs=[in_vmem(), in_vmem(), in_hbm()],
        out_specs=[in_vmem()] * 6,
        out_shape=[
            SHAPE(packed.shape, BF16),
            SHAPE((hidden, rows), F32),
            SHAPE((hidden, rows), F32),
            SHAPE((model, rows), F32),
            SHAPE((1, rows), F32),
            SHAPE((model, rows), F32),
        ],
        scratch_shapes=[pltpu.SemaphoreType.DMA((2 * steps + 1,))],
        compiler_params=params(),
        cost_estimate=cost(4 * rows * model * hidden, 12 * model * hidden, rows * hidden),
        name="block_forward",
    )(block_in, gain, packed)


def pack_half(value, half):
    middle = value.shape[0] // 2
    lane = lax.broadcasted_iota(jnp.int32, (middle, value.shape[1]), 1)
    own = (lane < value.shape[1] // 2) == (half == 0)
    return jnp.where(own, value[:middle, :], pltpu.roll(value[middle:, :], value.shape[1] // 2, 1))


def unpack_half(packed):
    packed = packed.astype(F32)
    return jnp.concatenate([packed, pltpu.roll(packed, packed.shape[1] // 2, 1)], axis=0)


def merge_halves(first, second):
    lane = lax.broadcasted_iota(jnp.int32, first.shape, 1)
    return jnp.where(lane < first.shape[1] // 2, first, second)


def block_backward(grad, state, earlier, turn, half, shard_rows, down_rows, height=384):
    held, gate_factor, _, xhat = state[:4]
    model, rows = xhat.shape
    hidden = gate_factor.shape[0]
    devices, _, lanes = held.shape
    steps = hidden // lanes
    chunks = model // lanes
    holders = lanes // down_rows
    down_start = 2 * steps * shard_rows
    final = bool(earlier)

    def compute(g_ref, w_ref, a_ref, b_ref, x_ref, inv_ref, gain_ref, dgate, dup, scaled):
        for j in range(steps):
            span = slice(j * lanes, (j + 1) * lanes)
            dmid = jnp.zeros((lanes, rows), F32)
            for c in range(chunks):
                part = slice(down_start + c * down_rows, down_start + (c + 1) * down_rows)
                down = w_ref[j * holders : (j + 1) * holders, part, :].reshape(lanes, lanes)
                dmid += jnp.dot(down, g_ref[c * lanes : (c + 1) * lanes, :], preferred_element_type=F32)
            dgate[span, :] = (dmid * a_ref[span, :]).astype(BF16)
            dup[span, :] = (dmid * b_ref[span, :]).astype(BF16)
        sum_e = jnp.zeros((1, rows), F32)
        sum_ex = jnp.zeros((1, rows), F32)
        count = height // shard_rows
        for n in range(0, devices, count):
            dz = jnp.zeros((height, rows), F32)
            for j in range(steps):
                span = slice(j * lanes, (j + 1) * lanes)
                for factor, start in ((dgate, j), (dup, steps + j)):
                    part = slice(start * shard_rows, (start + 1) * shard_rows)
                    weights = w_ref[n : n + count, part, :].reshape(height, lanes)
                    dz += jnp.dot(weights, factor[span, :], preferred_element_type=F32)
            place = slice(n * shard_rows, n * shard_rows + height)
            e = dz * gain_ref[place, :]
            scaled[place, :] = e
            sum_e += jnp.sum(e, axis=0, keepdims=True)
            sum_ex += jnp.sum(e * x_ref[place, :], axis=0, keepdims=True)
        inner = scaled[...] - sum_e / model - x_ref[...] * (sum_ex / model)
        return g_ref[...].astype(F32) + inv_ref[...] * inner

    def kernel(g_ref, *refs):
        state_refs, earlier_refs, out_ref = refs[:6], refs[6 : 6 + len(earlier)], refs[6 + len(earlier)]
        whole, *scratch = refs[-4:]
        section = lax.axis_index("section")

        @pl.when(section == turn)
        def _():
            if grad.shape[0] < model:
                whole[...] = unpack_half(g_ref[...]).astype(BF16)
            else:
                whole[...] = g_ref[...]
            result = compute(whole, *state_refs, *scratch)
            if final:
                out_ref[...] = merge_halves(unpack_half(earlier_refs[-1][...]), result).T.astype(BF16)
            else:
                out_ref[...] = pack_half(result, half).astype(BF16)

        if final:
            for before in range(3 - turn):

                @pl.when(section == 3 - before)
                def _():
                    halves = [unpack_half(ref[...]) for ref in earlier_refs[2 * before : 2 * before + 2]]
                    out_ref[...] = merge_halves(*halves).T.astype(BF16)
        else:

            @pl.when(section != turn)
            def _():
                out_ref[...] = jnp.zeros_like(out_ref)

    return pl.pallas_call(
        kernel,
        in_specs=[in_vmem()] * (7 + len(earlier)),
        out_specs=[in_vmem()] * (1 if final else 7),
        out_shape=[SHAPE((rows, model) if final else (model // 2, rows), BF16)]
        + ([] if final else [SHAPE(a.shape, a.dtype) for a in state]),
        input_output_aliases={} if final else {i: i for i in range(1, 7)},
        scratch_shapes=[
            pltpu.VMEM((model, rows), BF16),
            pltpu.VMEM((hidden, rows), BF16),
            pltpu.VMEM((hidden, rows), BF16),
            pltpu.VMEM((model, rows), F32),
        ],
        compiler_params=params(),
        cost_estimate=cost(6 * rows * model * hidden, 6 * model * hidden),
        name="block_backward",
    )(grad, *state, *earlier)


def after(value, *others):
    return lax.optimization_barrier((value, *others))[0]


def dp_pairs(move):
    pairs = []
    for i in range(32):
        z, x, core = move(i // 8, i // 2 % 4, i % 2)
        pairs.append((i, (z % 4 * 4 + x % 4) * 2 + core))
    return pairs


STAGES = (
    [lambda z, x, c, k=k: (z, x + k, c) for k in (1, 3, 2)],
    [lambda z, x, c, k=k: (z + k, x, c) for k in (1, 3, 2)],
)


def sum_over_dp(value, meanwhile=(None, None)):
    value = value + lax.ppermute(value, "dp", dp_pairs(lambda z, x, c: (z, x, 1 - c)))
    parts = None
    for moves, work in zip(STAGES, meanwhile):
        if parts is not None:
            value = (parts[0] + parts[1].astype(F32)) + (parts[2].astype(F32) + parts[3].astype(F32))
        small = value.astype(BF16)
        parts = [value] + [lax.ppermute(small, "dp", dp_pairs(move)) for move in moves]
        if work is not None:
            parts[3] = after(parts[3], work(small))
    return parts


def parts_over_section(value):
    return [value] + [
        lax.ppermute(value, "section", [(i, (i + k) % 4) for i in range(4)]) for k in (1, 3, 2)
    ]


def parts_to_last_section(value):
    return [value] + [lax.ppermute(value, "section", [(i, 3)]) for i in (2, 0, 1)]


def per_device(
    teacher_logits, prototypes, head_weight, student_out, block_inputs, ln_gain, w_gate, w_up, w_down
):
    packed = lax.all_gather(pack_weights(w_gate[0], w_up[0], w_down[0], 512), "dp", axis=0)
    hidden = w_gate.shape[2]
    shard_rows, down_rows = w_gate.shape[1], w_down.shape[1]

    logits = teacher_logits
    made = {}

    def make_unit(token):
        made["unit"], made["radius"] = student_unit(after(student_out, token), head_weight)
        return made["unit"]

    def first_half(token):
        made["student"], made["p"] = student_products(after(made["unit"], token), prototypes, None, 0, 2)
        return made["student"]

    def second_half(token):
        made["student"], made["p"] = student_products(
            after(made["unit"], token), made["p"], made["student"], 1, 2
        )
        return made["student"]

    def first_hop(token):
        student = after(made["student"], token)
        made["student"] = student + lax.ppermute(student, "section", [(1, 2), (0, 3)])
        return made["student"]

    def second_hop(token):
        student = after(made["student"], token)
        made["parts"] = [student, lax.ppermute(student, "section", [(2, 3)])]
        return made["parts"][1]

    sums, logits = column_sums(logits, [])
    column_parts = sum_over_dp(sums, (make_unit, first_half))
    sums, logits = row_sums(logits, column_parts)
    sums, logits = column_sums(logits, parts_over_section(sums))
    column_parts = sum_over_dp(sums, (second_half, first_hop))
    sums, logits = row_sums(logits, column_parts)
    sums, logits = column_sums(logits, parts_over_section(sums))
    column_parts = sum_over_dp(sums, (second_hop, None))
    target = target_products(logits, column_parts, made["p"])
    target_parts = parts_to_last_section(target)

    state = block_forward(after(block_inputs[0], target), ln_gain, packed, shard_rows, hidden)
    unit = after(made["unit"], state[4])
    incoming = head_gradient(made["parts"], target_parts, unit, made["radius"], head_weight)

    results = []
    grads = [incoming, incoming]
    for turn in (3, 2, 1, 0):
        for half in (0, 1):
            earlier = results if (turn, half) == (0, 1) else []
            computed, *state = block_backward(grads[half], state, earlier, turn, half, shard_rows, down_rows)
            results.append(computed)
            if turn:
                grads[half] = lax.ppermute(computed, "section", [(turn, turn - 1)])
    return computed[None]


def solution(mesh):
    in_specs = (
        P("dp", "section"),
        P("section", None),
        P(),
        P("dp", None),
        P("section", "dp", None),
        P("section", None),
        P("section", "dp", None),
        P("section", "dp", None),
        P("section", "dp", None),
    )
    out_specs = P("section", "dp", None)
    return jax.shard_map(per_device, mesh=mesh, in_specs=in_specs, out_specs=out_specs, check_vma=False)
```

```python
import math

import jax
import jax.numpy as jnp
from jax import lax
from jax.experimental import pallas as pl
from jax.experimental.pallas import tpu as pltpu
from jax.sharding import PartitionSpec as P

TEACHER_SCALE = 1.0 / 0.07
STUDENT_SCALE = 1.0 / 0.1
EPS = 1e-06
N_ITER = 3
F32 = jnp.float32
BF16 = jnp.bfloat16
NT = (((1,), (1,)), ((), ()))
LOG2E = math.log2(math.e)
VMEM_LIMIT = 16 * 1024 * 1024
LOGITS_LIMIT = 48 * 1024 * 1024
PROTOTYPES_LIMIT = 43 * 1024 * 1024
PACK_LIMIT = 55 * 1024 * 1024
SHAPE = jax.ShapeDtypeStruct


def params(limit=VMEM_LIMIT):
    return pltpu.CompilerParams(vmem_limit_bytes=limit)


def cost(flops, size, transcendentals=0):
    return pl.CostEstimate(flops=flops, bytes_accessed=size, transcendentals=transcendentals)


def in_hbm():
    return pl.BlockSpec(memory_space=pltpu.HBM)


def in_vmem():
    return pl.BlockSpec(memory_space=pltpu.VMEM)


def row_to_column(row):
    n = row.shape[1]
    eye = lax.broadcasted_iota(jnp.int32, (n, n), 0) == lax.broadcasted_iota(jnp.int32, (n, n), 1)
    return jnp.sum(jnp.where(eye, row, 0.0), axis=1, keepdims=True)


def column_to_row(column):
    n = column.shape[0]
    eye = lax.broadcasted_iota(jnp.int32, (n, n), 0) == lax.broadcasted_iota(jnp.int32, (n, n), 1)
    return jnp.sum(jnp.where(eye, column, 0.0), axis=0, keepdims=True)


def teacher_weights(logits):
    return jnp.exp2(logits.astype(F32) * (TEACHER_SCALE * LOG2E))


def add_all(refs):
    values = [ref[...].astype(F32) for ref in refs]
    while len(values) > 1:
        values = [a + b for a, b in zip(values[::2], values[1::2])] + values[len(values) & ~1 :]
    return values[0]


def lane_sums(value):
    parts = [value[:, k : k + 128] for k in range(0, value.shape[1], 128)]
    while len(parts) > 1:
        parts = [a + b for a, b in zip(parts[::2], parts[1::2])] + parts[len(parts) & ~1 :]
    return parts[0]


def first_column_sums(logits, width=1024):
    rows, columns = logits.shape
    steps = columns // width

    def kernel(l_ref, out_ref, held, sems):
        copies = [
            pltpu.make_async_copy(
                l_ref.at[:, pl.ds(k * width, width)], held.at[:, pl.ds(k * width, width)], sems.at[k]
            )
            for k in range(steps)
        ]
        for copy in copies:
            copy.start()
        for k in range(steps):
            copies[k].wait()
            weights = teacher_weights(held[:, k * width : (k + 1) * width])
            out_ref[k : k + 1, :] = jnp.sum(weights, axis=0, keepdims=True)

    return pl.pallas_call(
        kernel,
        in_specs=[in_hbm()],
        out_specs=[in_vmem()] * 2,
        out_shape=[SHAPE((steps, width), F32), SHAPE(logits.shape, BF16)],
        scratch_shapes=[pltpu.SemaphoreType.DMA((steps,))],
        compiler_params=params(LOGITS_LIMIT),
        cost_estimate=cost(4 * rows * columns, 2 * rows * columns, rows * columns),
        name="first_column_sums",
    )(logits)


def column_sums(weights, row_parts, width=1024):
    rows, columns = weights.shape
    steps = columns // width

    def kernel(w_ref, *refs):
        out_ref = refs[-2]
        scale = jnp.broadcast_to(row_to_column(1.0 / add_all(refs[:-2])), (rows, 128))
        scale = jnp.concatenate([scale] * (width // 128), axis=1)
        for k in range(steps):
            scaled = w_ref[:, k * width : (k + 1) * width] * scale
            out_ref[k : k + 1, :] = jnp.sum(scaled, axis=0, keepdims=True)

    return pl.pallas_call(
        kernel,
        in_specs=[in_vmem()] * (1 + len(row_parts)),
        out_specs=[in_vmem()] * 2,
        out_shape=[SHAPE((steps, width), F32), SHAPE(weights.shape, F32)],
        input_output_aliases={0: 1},
        compiler_params=params(),
        cost_estimate=cost(2 * rows * columns, 4 * rows * columns),
        name="column_sums",
    )(weights, *row_parts)


def row_sums(weights, column_parts):
    rows, columns = weights.shape
    width = column_parts[0].shape[1]
    first = weights.dtype == BF16

    def kernel(w_ref, *refs):
        out_ref, held = refs[-2:]
        scale = 1.0 / add_all(refs[:-2])
        total = jnp.zeros((rows, 128), F32)
        for k in range(columns // width):
            span = slice(k * width, (k + 1) * width)
            values = w_ref[:, span]
            if first:
                values = teacher_weights(values)
                held[:, span] = values
            total += lane_sums(values * scale[k : k + 1, :])
        out_ref[...] = column_to_row(jnp.sum(total, axis=1, keepdims=True))

    return pl.pallas_call(
        kernel,
        in_specs=[in_vmem()] * (1 + len(column_parts)),
        out_specs=[in_vmem()] * 2,
        out_shape=[SHAPE((1, rows), F32), SHAPE(weights.shape, F32)],
        input_output_aliases={} if first else {0: 1},
        compiler_params=params(),
        cost_estimate=cost(2 * rows * columns, 6 * rows * columns),
        name="row_sums",
    )(weights, *column_parts)


def target_products(weights, column_parts, prototypes):
    rows, columns = weights.shape
    width = column_parts[0].shape[1]
    bottleneck = prototypes.shape[1]

    def kernel(w_ref, p_ref, *refs):
        out_ref = refs[-1]
        scale = 1.0 / add_all(refs[:-1])
        total = jnp.zeros((rows, 128), F32)
        acc = jnp.zeros((rows, bottleneck), F32)
        for k in range(columns // width):
            span = slice(k * width, (k + 1) * width)
            scaled = w_ref[:, span] * scale[k : k + 1, :]
            total += lane_sums(scaled)
            acc += jnp.dot(scaled.astype(BF16), p_ref[span, :], preferred_element_type=F32)
        out_ref[:rows, :] = acc
        sums = column_to_row(jnp.sum(total, axis=1, keepdims=True))
        out_ref[rows:, :] = jnp.broadcast_to(jnp.concatenate([sums, sums], axis=1), (8, bottleneck))

    return pl.pallas_call(
        kernel,
        in_specs=[in_vmem()] * (2 + len(column_parts)),
        out_specs=in_vmem(),
        out_shape=SHAPE((rows + 8, bottleneck), F32),
        compiler_params=params(),
        cost_estimate=cost(2 * rows * columns * bottleneck, 16 * 1024 * 1024),
        name="target_products",
    )(weights, prototypes, *column_parts)


def student_unit(student_out, head):
    rows, model = student_out.shape
    bottleneck = head.shape[1]

    def kernel(s_ref, h_ref, unit_ref, radius_ref):
        feature = jnp.dot(s_ref[...], h_ref[...], preferred_element_type=F32)
        radius = jnp.sqrt(jnp.sum(feature * feature, axis=1, keepdims=True) + EPS)
        unit_ref[...] = feature / radius
        radius_ref[...] = jnp.broadcast_to(radius, radius_ref.shape)

    return pl.pallas_call(
        kernel,
        in_specs=[in_vmem()] * 2,
        out_specs=[in_vmem()] * 2,
        out_shape=[SHAPE((rows, bottleneck), F32), SHAPE((rows, 128), F32)],
        compiler_params=params(),
        cost_estimate=cost(2 * rows * model * bottleneck, 2 * 1024 * 1024),
        name="student_unit",
    )(student_out, head)


def student_products(unit, prototypes, before, part, parts, width=2048):
    rows, bottleneck = unit.shape
    columns = prototypes.shape[0]
    span = columns // parts
    first = before is None

    def kernel(u_ref, p_ref, *refs):
        if first:
            out_ref, held, sems = refs
            copies = [
                pltpu.make_async_copy(p_ref.at[pl.ds(k, width), :], held.at[pl.ds(k, width), :], sems.at[n])
                for n, k in enumerate(range(0, columns, width))
            ]
            for copy in copies:
                copy.start()
        else:
            before_ref, out_ref, _ = refs
            held = p_ref
        unit_b = u_ref[...].astype(BF16)
        total = jnp.zeros((rows, 128), F32)
        acc = jnp.zeros((rows, bottleneck), F32)
        for k in range(part * span, (part + 1) * span, width):
            if first:
                copies[k // width].wait()
            block = held[k : k + width, :]
            scores = lax.dot_general(unit_b, block, NT, preferred_element_type=F32)
            expo = jnp.exp2(scores * (STUDENT_SCALE * LOG2E))
            total += lane_sums(expo)
            acc += jnp.dot(expo.astype(BF16), block, preferred_element_type=F32)
        sums = column_to_row(jnp.sum(total, axis=1, keepdims=True))
        sums = jnp.broadcast_to(jnp.concatenate([sums, sums], axis=1), (8, bottleneck))
        if first:
            for copy in copies[span // width :]:
                copy.wait()
        else:
            acc += before_ref[:rows, :]
            sums += before_ref[rows:, :]
        out_ref[:rows, :] = acc
        out_ref[rows:, :] = sums

    return pl.pallas_call(
        kernel,
        in_specs=[in_vmem(), in_hbm() if first else in_vmem()]
        + ([] if first else [in_vmem()]),
        out_specs=[in_vmem()] * 2,
        out_shape=[SHAPE((rows + 8, bottleneck), F32), SHAPE(prototypes.shape, BF16)],
        input_output_aliases={} if first else {1: 1},
        scratch_shapes=[pltpu.SemaphoreType.DMA((columns // width,))] if first else [],
        compiler_params=params(PROTOTYPES_LIMIT if first else VMEM_LIMIT),
        cost_estimate=cost(4 * rows * span * bottleneck, 512 * span, rows * span),
        name="student_products",
    )(unit, prototypes, *([] if first else [before]))


def head_gradient(student_parts, target_parts, unit, radius, head):
    rows, bottleneck = unit.shape
    model = head.shape[0]
    count, total = len(student_parts), len(student_parts) + len(target_parts)

    def kernel(*refs):
        unit_ref, radius_ref, h_ref, out_ref = refs[total:]
        student = add_all(refs[:count])
        target = add_all(refs[count:total])
        dunit = (
            student[:rows, :] / row_to_column(student[rows : rows + 1, :rows])
            - target[:rows, :] / row_to_column(target[rows : rows + 1, :rows])
        ) * STUDENT_SCALE
        unit = unit_ref[...]
        along = jnp.sum(unit * dunit, axis=1, keepdims=True)
        dfeature = ((dunit - unit * along) / radius_ref[:, :1]).astype(BF16)
        out_ref[...] = lax.dot_general(h_ref[...], dfeature, NT, preferred_element_type=F32).astype(BF16)

    parts = list(student_parts) + list(target_parts)
    return pl.pallas_call(
        kernel,
        in_specs=[in_vmem()] * (total + 3),
        out_specs=in_vmem(),
        out_shape=SHAPE((model, rows), BF16),
        compiler_params=params(),
        cost_estimate=cost(2 * rows * model * bottleneck, 3 * 1024 * 1024),
        name="head_gradient",
    )(*parts, unit, radius, head)


def pack_weights(w_gate, w_up, w_down, lanes):
    arrays = (w_gate, w_up, w_down)

    moves = []
    row = 0
    for index, w in enumerate(arrays):
        for k in range(0, w.shape[1], lanes):
            moves.append((index, k, row, w.shape[0]))
            row += w.shape[0]

    def kernel(*refs):
        out_ref, sems = refs[-2:]
        copies = [
            pltpu.make_async_copy(
                refs[index].at[:, pl.ds(k, lanes)], out_ref.at[pl.ds(row, height), :], sems.at[n]
            )
            for n, (index, k, row, height) in enumerate(moves)
        ]
        for copy in copies:
            copy.start()
        for copy in copies:
            copy.wait()

    total = sum(w.shape[0] * w.shape[1] for w in arrays)
    return pl.pallas_call(
        kernel,
        in_specs=[in_hbm()] * 3,
        out_specs=in_vmem(),
        out_shape=SHAPE((total // lanes, lanes), BF16),
        scratch_shapes=[pltpu.SemaphoreType.DMA((len(moves),))],
        compiler_params=params(PACK_LIMIT),
        cost_estimate=cost(0, 4 * total),
        name="pack_weights",
    )(*arrays)


def block_forward(block_in, gain, packed, shard_rows, hidden):
    rows, model = block_in.shape
    devices, height, lanes = packed.shape
    steps = hidden // lanes

    def kernel(x_ref, gain_ref, w_ref, held, a_ref, b_ref, xhat_ref, inverse_ref, gain_out, sems):
        def copy(k):
            if k < 2 * steps:
                part = pl.ds(k * shard_rows, shard_rows)
            else:
                part = pl.ds(2 * steps * shard_rows, height - 2 * steps * shard_rows)
            return pltpu.make_async_copy(w_ref.at[:, part, :], held.at[:, part, :], sems.at[k])

        order = [k for j in range(steps) for k in (j, steps + j)] + [2 * steps]
        for k in order:
            copy(k).start()
        xfloat = x_ref[...].astype(F32)
        centered = xfloat - jnp.mean(xfloat, axis=1, keepdims=True)
        inverse = lax.rsqrt(jnp.mean(centered * centered, axis=1, keepdims=True) + EPS)
        xhat = centered * inverse
        z = (xhat * gain_ref[...]).astype(BF16)
        xhat_ref[...] = xhat.T
        inverse_ref[...] = column_to_row(inverse)
        gain_out[...] = jnp.broadcast_to(gain_ref[...], (rows, model)).T
        for j in range(steps):
            copy(j).wait()
            copy(steps + j).wait()
            gate_w = held[:, j * shard_rows : (j + 1) * shard_rows, :].reshape(model, lanes)
            up_w = held[:, (steps + j) * shard_rows : (steps + j + 1) * shard_rows, :].reshape(model, lanes)
            gate = jnp.dot(z, gate_w, preferred_element_type=F32)
            up = jnp.dot(z, up_w, preferred_element_type=F32)
            sigma = 1.0 / (1.0 + jnp.exp(-gate))
            a_ref[j * lanes : (j + 1) * lanes, :] = (up * sigma * (1.0 + gate * (1.0 - sigma))).T
            b_ref[j * lanes : (j + 1) * lanes, :] = (gate * sigma).T
        copy(2 * steps).wait()

    return pl.pallas_call(
        kernel,
        in_specs=[in_vmem(), in_vmem(), in_hbm()],
        out_specs=[in_vmem()] * 6,
        out_shape=[
            SHAPE(packed.shape, BF16),
            SHAPE((hidden, rows), F32),
            SHAPE((hidden, rows), F32),
            SHAPE((model, rows), F32),
            SHAPE((1, rows), F32),
            SHAPE((model, rows), F32),
        ],
        scratch_shapes=[pltpu.SemaphoreType.DMA((2 * steps + 1,))],
        compiler_params=params(),
        cost_estimate=cost(4 * rows * model * hidden, 12 * model * hidden, rows * hidden),
        name="block_forward",
    )(block_in, gain, packed)


def pack_half(value, half):
    middle = value.shape[0] // 2
    lane = lax.broadcasted_iota(jnp.int32, (middle, value.shape[1]), 1)
    own = (lane < value.shape[1] // 2) == (half == 0)
    return jnp.where(own, value[:middle, :], pltpu.roll(value[middle:, :], value.shape[1] // 2, 1))


def unpack_half(packed):
    packed = packed.astype(F32)
    return jnp.concatenate([packed, pltpu.roll(packed, packed.shape[1] // 2, 1)], axis=0)


def merge_halves(first, second):
    lane = lax.broadcasted_iota(jnp.int32, first.shape, 1)
    return jnp.where(lane < first.shape[1] // 2, first, second)


def block_backward(grad, state, earlier, turn, half, shard_rows, down_rows, height=384):
    held, gate_factor, _, xhat = state[:4]
    model, rows = xhat.shape
    hidden = gate_factor.shape[0]
    devices, _, lanes = held.shape
    steps = hidden // lanes
    chunks = model // lanes
    holders = lanes // down_rows
    down_start = 2 * steps * shard_rows
    final = bool(earlier)

    def compute(g_ref, w_ref, a_ref, b_ref, x_ref, inv_ref, gain_ref, dgate, dup, scaled):
        for j in range(steps):
            span = slice(j * lanes, (j + 1) * lanes)
            dmid = jnp.zeros((lanes, rows), F32)
            for c in range(chunks):
                part = slice(down_start + c * down_rows, down_start + (c + 1) * down_rows)
                down = w_ref[j * holders : (j + 1) * holders, part, :].reshape(lanes, lanes)
                dmid += jnp.dot(down, g_ref[c * lanes : (c + 1) * lanes, :], preferred_element_type=F32)
            dgate[span, :] = (dmid * a_ref[span, :]).astype(BF16)
            dup[span, :] = (dmid * b_ref[span, :]).astype(BF16)
        sum_e = jnp.zeros((1, rows), F32)
        sum_ex = jnp.zeros((1, rows), F32)
        count = height // shard_rows
        for n in range(0, devices, count):
            dz = jnp.zeros((height, rows), F32)
            for j in range(steps):
                span = slice(j * lanes, (j + 1) * lanes)
                for factor, start in ((dgate, j), (dup, steps + j)):
                    part = slice(start * shard_rows, (start + 1) * shard_rows)
                    weights = w_ref[n : n + count, part, :].reshape(height, lanes)
                    dz += jnp.dot(weights, factor[span, :], preferred_element_type=F32)
            place = slice(n * shard_rows, n * shard_rows + height)
            e = dz * gain_ref[place, :]
            scaled[place, :] = e
            sum_e += jnp.sum(e, axis=0, keepdims=True)
            sum_ex += jnp.sum(e * x_ref[place, :], axis=0, keepdims=True)
        inner = scaled[...] - sum_e / model - x_ref[...] * (sum_ex / model)
        return g_ref[...].astype(F32) + inv_ref[...] * inner

    def kernel(g_ref, *refs):
        state_refs, earlier_refs, out_ref = refs[:6], refs[6 : 6 + len(earlier)], refs[6 + len(earlier)]
        whole, *scratch = refs[-4:]
        section = lax.axis_index("section")

        @pl.when(section == turn)
        def _():
            if grad.shape[0] < model:
                whole[...] = unpack_half(g_ref[...]).astype(BF16)
            else:
                whole[...] = g_ref[...]
            result = compute(whole, *state_refs, *scratch)
            if final:
                out_ref[...] = merge_halves(unpack_half(earlier_refs[-1][...]), result).T.astype(BF16)
            else:
                out_ref[...] = pack_half(result, half).astype(BF16)

        if final:
            for before in range(3 - turn):

                @pl.when(section == 3 - before)
                def _():
                    halves = [unpack_half(ref[...]) for ref in earlier_refs[2 * before : 2 * before + 2]]
                    out_ref[...] = merge_halves(*halves).T.astype(BF16)
        else:

            @pl.when(section != turn)
            def _():
                out_ref[...] = jnp.zeros_like(out_ref)

    return pl.pallas_call(
        kernel,
        in_specs=[in_vmem()] * (7 + len(earlier)),
        out_specs=[in_vmem()] * (1 if final else 7),
        out_shape=[SHAPE((rows, model) if final else (model // 2, rows), BF16)]
        + ([] if final else [SHAPE(a.shape, a.dtype) for a in state]),
        input_output_aliases={} if final else {i: i for i in range(1, 7)},
        scratch_shapes=[
            pltpu.VMEM((model, rows), BF16),
            pltpu.VMEM((hidden, rows), BF16),
            pltpu.VMEM((hidden, rows), BF16),
            pltpu.VMEM((model, rows), F32),
        ],
        compiler_params=params(),
        cost_estimate=cost(6 * rows * model * hidden, 6 * model * hidden),
        name="block_backward",
    )(grad, *state, *earlier)


def after(value, *others):
    return lax.optimization_barrier((value, *others))[0]


def dp_pairs(move):
    pairs = []
    for i in range(32):
        z, x, core = move(i // 8, i // 2 % 4, i % 2)
        pairs.append((i, (z % 4 * 4 + x % 4) * 2 + core))
    return pairs


STAGES = (
    [lambda z, x, c, k=k: (z, x + k, c) for k in (1, 3, 2)],
    [lambda z, x, c, k=k: (z + k, x, c) for k in (1, 3, 2)],
)


def sum_over_dp(value, meanwhile=(None, None)):
    value = value + lax.ppermute(value, "dp", dp_pairs(lambda z, x, c: (z, x, 1 - c)))
    parts = None
    for moves, work in zip(STAGES, meanwhile):
        if parts is not None:
            value = (parts[0] + parts[1].astype(F32)) + (parts[2].astype(F32) + parts[3].astype(F32))
        small = value.astype(BF16)
        parts = [value] + [lax.ppermute(small, "dp", dp_pairs(move)) for move in moves]
        if work is not None:
            parts[3] = after(parts[3], work(small))
    return parts


def parts_over_section(value):
    return [value] + [
        lax.ppermute(value, "section", [(i, (i + k) % 4) for i in range(4)]) for k in (1, 3, 2)
    ]


def parts_to_last_section(value):
    return [value] + [lax.ppermute(value, "section", [(i, 3)]) for i in (2, 0, 1)]


def per_device(
    teacher_logits, prototypes, head_weight, student_out, block_inputs, ln_gain, w_gate, w_up, w_down
):
    packed = lax.all_gather(pack_weights(w_gate[0], w_up[0], w_down[0], 512), "dp", axis=0)
    hidden = w_gate.shape[2]
    shard_rows, down_rows = w_gate.shape[1], w_down.shape[1]

    made = {}

    def make_unit(token):
        made["unit"], made["radius"] = student_unit(after(student_out, token), head_weight)
        return made["unit"]

    def first_half(token):
        made["student"], made["p"] = student_products(after(made["unit"], token), prototypes, None, 0, 2)
        return made["student"]

    def second_half(token):
        made["student"], made["p"] = student_products(
            after(made["unit"], token), made["p"], made["student"], 1, 2
        )
        return made["student"]

    def first_hop(token):
        student = after(made["student"], token)
        made["student"] = student + lax.ppermute(student, "section", [(1, 2), (0, 3)])
        return made["student"]

    def second_hop(token):
        student = after(made["student"], token)
        made["parts"] = [student, lax.ppermute(student, "section", [(2, 3)])]
        return made["parts"][1]

    sums, logits = first_column_sums(teacher_logits)
    column_parts = sum_over_dp(sums, (make_unit, first_half))
    sums, weights = row_sums(logits, column_parts)
    sums, weights = column_sums(weights, parts_over_section(sums))
    column_parts = sum_over_dp(sums, (second_half, first_hop))
    sums, weights = row_sums(weights, column_parts)
    sums, weights = column_sums(weights, parts_over_section(sums))
    column_parts = sum_over_dp(sums, (second_hop, None))
    target = target_products(weights, column_parts, made["p"])
    target_parts = parts_to_last_section(target)

    state = block_forward(after(block_inputs[0], target), ln_gain, packed, shard_rows, hidden)
    unit = after(made["unit"], state[4])
    incoming = head_gradient(made["parts"], target_parts, unit, made["radius"], head_weight)

    results = []
    grads = [incoming, incoming]
    for turn in (3, 2, 1, 0):
        for half in (0, 1):
            earlier = results if (turn, half) == (0, 1) else []
            computed, *state = block_backward(grads[half], state, earlier, turn, half, shard_rows, down_rows)
            results.append(computed)
            if turn:
                grads[half] = lax.ppermute(computed, "section", [(turn, turn - 1)])
    return computed[None]


def solution(mesh):
    in_specs = (
        P("dp", "section"),
        P("section", None),
        P(),
        P("dp", None),
        P("section", "dp", None),
        P("section", None),
        P("section", "dp", None),
        P("section", "dp", None),
        P("section", "dp", None),
    )
    out_specs = P("section", "dp", None)
    return jax.shard_map(per_device, mesh=mesh, in_specs=in_specs, out_specs=out_specs, check_vma=False)
```

```python
import math

import jax
import jax.numpy as jnp
from jax import lax
from jax.experimental import pallas as pl
from jax.experimental.pallas import tpu as pltpu
from jax.sharding import PartitionSpec as P

TEACHER_SCALE = 1.0 / 0.07
STUDENT_SCALE = 1.0 / 0.1
EPS = 1e-06
N_ITER = 3
F32 = jnp.float32
BF16 = jnp.bfloat16
NT = (((1,), (1,)), ((), ()))
LOG2E = math.log2(math.e)
VMEM_LIMIT = 16 * 1024 * 1024
LOGITS_LIMIT = 48 * 1024 * 1024
PROTOTYPES_LIMIT = 43 * 1024 * 1024
PACK_LIMIT = 55 * 1024 * 1024
SHAPE = jax.ShapeDtypeStruct


def params(limit=VMEM_LIMIT):
    return pltpu.CompilerParams(vmem_limit_bytes=limit)


def cost(flops, size, transcendentals=0):
    return pl.CostEstimate(flops=flops, bytes_accessed=size, transcendentals=transcendentals)


def in_hbm():
    return pl.BlockSpec(memory_space=pltpu.HBM)


def in_vmem():
    return pl.BlockSpec(memory_space=pltpu.VMEM)


def row_to_column(row):
    n = row.shape[1]
    eye = lax.broadcasted_iota(jnp.int32, (n, n), 0) == lax.broadcasted_iota(jnp.int32, (n, n), 1)
    return jnp.sum(jnp.where(eye, row, 0.0), axis=1, keepdims=True)


def column_to_row(column):
    n = column.shape[0]
    eye = lax.broadcasted_iota(jnp.int32, (n, n), 0) == lax.broadcasted_iota(jnp.int32, (n, n), 1)
    return jnp.sum(jnp.where(eye, column, 0.0), axis=0, keepdims=True)


def teacher_weights(logits):
    return jnp.exp2(logits.astype(F32) * (TEACHER_SCALE * LOG2E))


def add_all(refs):
    values = [ref[...].astype(F32) for ref in refs]
    while len(values) > 1:
        values = [a + b for a, b in zip(values[::2], values[1::2])] + values[len(values) & ~1 :]
    return values[0]


def lane_sums(value):
    parts = [value[:, k : k + 128] for k in range(0, value.shape[1], 128)]
    while len(parts) > 1:
        parts = [a + b for a, b in zip(parts[::2], parts[1::2])] + parts[len(parts) & ~1 :]
    return parts[0]


def first_column_sums(logits, width=1024):
    rows, columns = logits.shape
    steps = columns // width

    def kernel(l_ref, out_ref, held, sems):
        copies = [
            pltpu.make_async_copy(
                l_ref.at[:, pl.ds(k * width, width)], held.at[:, pl.ds(k * width, width)], sems.at[k]
            )
            for k in range(steps)
        ]
        for copy in copies:
            copy.start()
        for k in range(steps):
            copies[k].wait()
            weights = teacher_weights(held[:, k * width : (k + 1) * width])
            out_ref[k : k + 1, :] = jnp.sum(weights, axis=0, keepdims=True)

    return pl.pallas_call(
        kernel,
        in_specs=[in_hbm()],
        out_specs=[in_vmem()] * 2,
        out_shape=[SHAPE((steps, width), F32), SHAPE(logits.shape, BF16)],
        scratch_shapes=[pltpu.SemaphoreType.DMA((steps,))],
        compiler_params=params(LOGITS_LIMIT),
        cost_estimate=cost(4 * rows * columns, 2 * rows * columns, rows * columns),
        name="first_column_sums",
    )(logits)


def column_sums(weights, row_parts, width=1024):
    rows, columns = weights.shape
    steps = columns // width

    def kernel(w_ref, *refs):
        out_ref = refs[-2]
        scale = jnp.broadcast_to(row_to_column(1.0 / add_all(refs[:-2])), (rows, 128))
        scale = jnp.concatenate([scale] * (width // 128), axis=1)
        for k in range(steps):
            scaled = w_ref[:, k * width : (k + 1) * width] * scale
            out_ref[k : k + 1, :] = jnp.sum(scaled, axis=0, keepdims=True)

    return pl.pallas_call(
        kernel,
        in_specs=[in_vmem()] * (1 + len(row_parts)),
        out_specs=[in_vmem()] * 2,
        out_shape=[SHAPE((steps, width), F32), SHAPE(weights.shape, F32)],
        input_output_aliases={0: 1},
        compiler_params=params(),
        cost_estimate=cost(2 * rows * columns, 4 * rows * columns),
        name="column_sums",
    )(weights, *row_parts)


def row_sums(weights, column_parts):
    rows, columns = weights.shape
    width = column_parts[0].shape[1]
    first = weights.dtype == BF16

    def kernel(w_ref, *refs):
        out_ref, held = refs[-2:]
        scale = 1.0 / add_all(refs[:-2])
        total = jnp.zeros((rows, 128), F32)
        for k in range(columns // width):
            span = slice(k * width, (k + 1) * width)
            values = w_ref[:, span]
            if first:
                values = teacher_weights(values)
                held[:, span] = values
            total += lane_sums(values * scale[k : k + 1, :])
        out_ref[...] = column_to_row(jnp.sum(total, axis=1, keepdims=True))

    return pl.pallas_call(
        kernel,
        in_specs=[in_vmem()] * (1 + len(column_parts)),
        out_specs=[in_vmem()] * 2,
        out_shape=[SHAPE((1, rows), F32), SHAPE(weights.shape, F32)],
        input_output_aliases={} if first else {0: 1},
        compiler_params=params(),
        cost_estimate=cost(2 * rows * columns, 6 * rows * columns),
        name="row_sums",
    )(weights, *column_parts)


def target_products(weights, column_parts, prototypes):
    rows, columns = weights.shape
    width = column_parts[0].shape[1]
    bottleneck = prototypes.shape[1]

    def kernel(w_ref, p_ref, *refs):
        out_ref = refs[-1]
        scale = 1.0 / add_all(refs[:-1])
        total = jnp.zeros((rows, 128), F32)
        acc = jnp.zeros((rows, bottleneck), F32)
        for k in range(columns // width):
            span = slice(k * width, (k + 1) * width)
            scaled = w_ref[:, span] * scale[k : k + 1, :]
            total += lane_sums(scaled)
            acc += jnp.dot(scaled.astype(BF16), p_ref[span, :], preferred_element_type=F32)
        out_ref[:rows, :] = acc
        sums = column_to_row(jnp.sum(total, axis=1, keepdims=True))
        out_ref[rows:, :] = jnp.broadcast_to(jnp.concatenate([sums, sums], axis=1), (8, bottleneck))

    return pl.pallas_call(
        kernel,
        in_specs=[in_vmem()] * (2 + len(column_parts)),
        out_specs=in_vmem(),
        out_shape=SHAPE((rows + 8, bottleneck), F32),
        compiler_params=params(),
        cost_estimate=cost(2 * rows * columns * bottleneck, 16 * 1024 * 1024),
        name="target_products",
    )(weights, prototypes, *column_parts)


def student_unit(student_out, head):
    rows, model = student_out.shape
    bottleneck = head.shape[1]

    def kernel(s_ref, h_ref, unit_ref, radius_ref):
        feature = jnp.dot(s_ref[...], h_ref[...], preferred_element_type=F32)
        radius = jnp.sqrt(jnp.sum(feature * feature, axis=1, keepdims=True) + EPS)
        unit_ref[...] = feature / radius
        radius_ref[...] = jnp.broadcast_to(radius, radius_ref.shape)

    return pl.pallas_call(
        kernel,
        in_specs=[in_vmem()] * 2,
        out_specs=[in_vmem()] * 2,
        out_shape=[SHAPE((rows, bottleneck), F32), SHAPE((rows, 128), F32)],
        compiler_params=params(),
        cost_estimate=cost(2 * rows * model * bottleneck, 2 * 1024 * 1024),
        name="student_unit",
    )(student_out, head)


def student_products(unit, prototypes, before, start, stop, width=2048):
    rows, bottleneck = unit.shape
    columns = prototypes.shape[0]
    span = stop - start
    first = before is None

    def kernel(u_ref, p_ref, *refs):
        if first:
            out_ref, held, sems = refs
            copies = [
                pltpu.make_async_copy(p_ref.at[pl.ds(k, width), :], held.at[pl.ds(k, width), :], sems.at[n])
                for n, k in enumerate(range(0, columns, width))
            ]
            for copy in copies:
                copy.start()
        else:
            before_ref, out_ref, _ = refs
            held = p_ref
        unit_b = u_ref[...].astype(BF16)
        total = jnp.zeros((rows, 128), F32)
        acc = jnp.zeros((rows, bottleneck), F32)
        for k in range(start, stop, width):
            if first:
                copies[k // width].wait()
            block = held[k : k + width, :]
            scores = lax.dot_general(unit_b, block, NT, preferred_element_type=F32)
            expo = jnp.exp2(scores * (STUDENT_SCALE * LOG2E))
            total += lane_sums(expo)
            acc += jnp.dot(expo.astype(BF16), block, preferred_element_type=F32)
        sums = column_to_row(jnp.sum(total, axis=1, keepdims=True))
        sums = jnp.broadcast_to(jnp.concatenate([sums, sums], axis=1), (8, bottleneck))
        if first:
            for copy in copies[span // width :]:
                copy.wait()
        else:
            acc += before_ref[:rows, :]
            sums += before_ref[rows:, :]
        out_ref[:rows, :] = acc
        out_ref[rows:, :] = sums

    return pl.pallas_call(
        kernel,
        in_specs=[in_vmem(), in_hbm() if first else in_vmem()]
        + ([] if first else [in_vmem()]),
        out_specs=[in_vmem()] * 2,
        out_shape=[SHAPE((rows + 8, bottleneck), F32), SHAPE(prototypes.shape, BF16)],
        input_output_aliases={} if first else {1: 1},
        scratch_shapes=[pltpu.SemaphoreType.DMA((columns // width,))] if first else [],
        compiler_params=params(PROTOTYPES_LIMIT if first else VMEM_LIMIT),
        cost_estimate=cost(4 * rows * span * bottleneck, 512 * span, rows * span),
        name="student_products",
    )(unit, prototypes, *([] if first else [before]))


def head_gradient(student_parts, target_parts, unit, radius, head):
    rows, bottleneck = unit.shape
    model = head.shape[0]
    count, total = len(student_parts), len(student_parts) + len(target_parts)

    def kernel(*refs):
        unit_ref, radius_ref, h_ref, out_ref = refs[total:]
        student = add_all(refs[:count])
        target = add_all(refs[count:total])
        dunit = (
            student[:rows, :] / row_to_column(student[rows : rows + 1, :rows])
            - target[:rows, :] / row_to_column(target[rows : rows + 1, :rows])
        ) * STUDENT_SCALE
        unit = unit_ref[...]
        along = jnp.sum(unit * dunit, axis=1, keepdims=True)
        dfeature = ((dunit - unit * along) / radius_ref[:, :1]).astype(BF16)
        out_ref[...] = lax.dot_general(h_ref[...], dfeature, NT, preferred_element_type=F32).astype(BF16)

    parts = list(student_parts) + list(target_parts)
    return pl.pallas_call(
        kernel,
        in_specs=[in_vmem()] * (total + 3),
        out_specs=in_vmem(),
        out_shape=SHAPE((model, rows), BF16),
        compiler_params=params(),
        cost_estimate=cost(2 * rows * model * bottleneck, 3 * 1024 * 1024),
        name="head_gradient",
    )(*parts, unit, radius, head)


def pack_weights(w_gate, w_up, w_down, lanes):
    arrays = (w_gate, w_up, w_down)

    moves = []
    row = 0
    for index, w in enumerate(arrays):
        for k in range(0, w.shape[1], lanes):
            moves.append((index, k, row, w.shape[0]))
            row += w.shape[0]

    def kernel(*refs):
        out_ref, sems = refs[-2:]
        copies = [
            pltpu.make_async_copy(
                refs[index].at[:, pl.ds(k, lanes)], out_ref.at[pl.ds(row, height), :], sems.at[n]
            )
            for n, (index, k, row, height) in enumerate(moves)
        ]
        for copy in copies:
            copy.start()
        for copy in copies:
            copy.wait()

    total = sum(w.shape[0] * w.shape[1] for w in arrays)
    return pl.pallas_call(
        kernel,
        in_specs=[in_hbm()] * 3,
        out_specs=in_vmem(),
        out_shape=SHAPE((total // lanes, lanes), BF16),
        scratch_shapes=[pltpu.SemaphoreType.DMA((len(moves),))],
        compiler_params=params(PACK_LIMIT),
        cost_estimate=cost(0, 4 * total),
        name="pack_weights",
    )(*arrays)


def block_forward(block_in, gain, packed, shard_rows, hidden):
    rows, model = block_in.shape
    devices, height, lanes = packed.shape
    steps = hidden // lanes

    def kernel(x_ref, gain_ref, w_ref, held, a_ref, b_ref, xhat_ref, inverse_ref, gain_out, sems):
        def copy(k):
            if k < 2 * steps:
                part = pl.ds(k * shard_rows, shard_rows)
            else:
                part = pl.ds(2 * steps * shard_rows, height - 2 * steps * shard_rows)
            return pltpu.make_async_copy(w_ref.at[:, part, :], held.at[:, part, :], sems.at[k])

        order = [k for j in range(steps) for k in (j, steps + j)] + [2 * steps]
        for k in order:
            copy(k).start()
        xfloat = x_ref[...].astype(F32)
        centered = xfloat - jnp.mean(xfloat, axis=1, keepdims=True)
        inverse = lax.rsqrt(jnp.mean(centered * centered, axis=1, keepdims=True) + EPS)
        xhat = centered * inverse
        z = (xhat * gain_ref[...]).astype(BF16)
        xhat_ref[...] = xhat.T
        inverse_ref[...] = column_to_row(inverse)
        gain_out[...] = jnp.broadcast_to(gain_ref[...], (rows, model)).T
        for j in range(steps):
            copy(j).wait()
            copy(steps + j).wait()
            gate_w = held[:, j * shard_rows : (j + 1) * shard_rows, :].reshape(model, lanes)
            up_w = held[:, (steps + j) * shard_rows : (steps + j + 1) * shard_rows, :].reshape(model, lanes)
            gate = jnp.dot(z, gate_w, preferred_element_type=F32)
            up = jnp.dot(z, up_w, preferred_element_type=F32)
            sigma = 1.0 / (1.0 + jnp.exp(-gate))
            a_ref[j * lanes : (j + 1) * lanes, :] = (up * sigma * (1.0 + gate * (1.0 - sigma))).T
            b_ref[j * lanes : (j + 1) * lanes, :] = (gate * sigma).T
        copy(2 * steps).wait()

    return pl.pallas_call(
        kernel,
        in_specs=[in_vmem(), in_vmem(), in_hbm()],
        out_specs=[in_vmem()] * 6,
        out_shape=[
            SHAPE(packed.shape, BF16),
            SHAPE((hidden, rows), F32),
            SHAPE((hidden, rows), F32),
            SHAPE((model, rows), F32),
            SHAPE((1, rows), F32),
            SHAPE((model, rows), F32),
        ],
        scratch_shapes=[pltpu.SemaphoreType.DMA((2 * steps + 1,))],
        compiler_params=params(),
        cost_estimate=cost(4 * rows * model * hidden, 12 * model * hidden, rows * hidden),
        name="block_forward",
    )(block_in, gain, packed)


def pack_half(value, half):
    middle = value.shape[0] // 2
    lane = lax.broadcasted_iota(jnp.int32, (middle, value.shape[1]), 1)
    own = (lane < value.shape[1] // 2) == (half == 0)
    return jnp.where(own, value[:middle, :], pltpu.roll(value[middle:, :], value.shape[1] // 2, 1))


def unpack_half(packed):
    packed = packed.astype(F32)
    return jnp.concatenate([packed, pltpu.roll(packed, packed.shape[1] // 2, 1)], axis=0)


def merge_halves(first, second):
    lane = lax.broadcasted_iota(jnp.int32, first.shape, 1)
    return jnp.where(lane < first.shape[1] // 2, first, second)


def block_backward(grad, state, earlier, turn, half, shard_rows, down_rows, height=384):
    held, gate_factor, _, xhat = state[:4]
    model, rows = xhat.shape
    hidden = gate_factor.shape[0]
    devices, _, lanes = held.shape
    steps = hidden // lanes
    chunks = model // lanes
    holders = lanes // down_rows
    down_start = 2 * steps * shard_rows
    final = bool(earlier)

    def compute(g_ref, w_ref, a_ref, b_ref, x_ref, inv_ref, gain_ref, dgate, dup, scaled):
        for j in range(steps):
            span = slice(j * lanes, (j + 1) * lanes)
            dmid = jnp.zeros((lanes, rows), F32)
            for c in range(chunks):
                part = slice(down_start + c * down_rows, down_start + (c + 1) * down_rows)
                down = w_ref[j * holders : (j + 1) * holders, part, :].reshape(lanes, lanes)
                dmid += jnp.dot(down, g_ref[c * lanes : (c + 1) * lanes, :], preferred_element_type=F32)
            dgate[span, :] = (dmid * a_ref[span, :]).astype(BF16)
            dup[span, :] = (dmid * b_ref[span, :]).astype(BF16)
        sum_e = jnp.zeros((1, rows), F32)
        sum_ex = jnp.zeros((1, rows), F32)
        count = height // shard_rows
        for n in range(0, devices, count):
            dz = jnp.zeros((height, rows), F32)
            for j in range(steps):
                span = slice(j * lanes, (j + 1) * lanes)
                for factor, start in ((dgate, j), (dup, steps + j)):
                    part = slice(start * shard_rows, (start + 1) * shard_rows)
                    weights = w_ref[n : n + count, part, :].reshape(height, lanes)
                    dz += jnp.dot(weights, factor[span, :], preferred_element_type=F32)
            place = slice(n * shard_rows, n * shard_rows + height)
            e = dz * gain_ref[place, :]
            scaled[place, :] = e
            sum_e += jnp.sum(e, axis=0, keepdims=True)
            sum_ex += jnp.sum(e * x_ref[place, :], axis=0, keepdims=True)
        inner = scaled[...] - sum_e / model - x_ref[...] * (sum_ex / model)
        return g_ref[...].astype(F32) + inv_ref[...] * inner

    def kernel(g_ref, *refs):
        state_refs, earlier_refs, out_ref = refs[:6], refs[6 : 6 + len(earlier)], refs[6 + len(earlier)]
        whole, *scratch = refs[-4:]
        section = lax.axis_index("section")

        @pl.when(section == turn)
        def _():
            if grad.shape[0] < model:
                whole[...] = unpack_half(g_ref[...]).astype(BF16)
            else:
                whole[...] = g_ref[...]
            result = compute(whole, *state_refs, *scratch)
            if final:
                out_ref[...] = merge_halves(unpack_half(earlier_refs[-1][...]), result).T.astype(BF16)
            else:
                out_ref[...] = pack_half(result, half).astype(BF16)

        if final:
            for before in range(3 - turn):

                @pl.when(section == 3 - before)
                def _():
                    halves = [unpack_half(ref[...]) for ref in earlier_refs[2 * before : 2 * before + 2]]
                    out_ref[...] = merge_halves(*halves).T.astype(BF16)
        else:

            @pl.when(section != turn)
            def _():
                out_ref[...] = jnp.zeros_like(out_ref)

    return pl.pallas_call(
        kernel,
        in_specs=[in_vmem()] * (7 + len(earlier)),
        out_specs=[in_vmem()] * (1 if final else 7),
        out_shape=[SHAPE((rows, model) if final else (model // 2, rows), BF16)]
        + ([] if final else [SHAPE(a.shape, a.dtype) for a in state]),
        input_output_aliases={} if final else {i: i for i in range(1, 7)},
        scratch_shapes=[
            pltpu.VMEM((model, rows), BF16),
            pltpu.VMEM((hidden, rows), BF16),
            pltpu.VMEM((hidden, rows), BF16),
            pltpu.VMEM((model, rows), F32),
        ],
        compiler_params=params(),
        cost_estimate=cost(6 * rows * model * hidden, 6 * model * hidden),
        name="block_backward",
    )(grad, *state, *earlier)


def after(value, *others):
    return lax.optimization_barrier((value, *others))[0]


def dp_pairs(move):
    pairs = []
    for i in range(32):
        z, x, core = move(i // 8, i // 2 % 4, i % 2)
        pairs.append((i, (z % 4 * 4 + x % 4) * 2 + core))
    return pairs


STAGES = (
    [lambda z, x, c, k=k: (z, x + k, c) for k in (1, 3, 2)],
    [lambda z, x, c, k=k: (z + k, x, c) for k in (1, 3, 2)],
)


def sum_over_dp(value, meanwhile=(None, None)):
    value = value + lax.ppermute(value, "dp", dp_pairs(lambda z, x, c: (z, x, 1 - c)))
    parts = None
    for moves, work in zip(STAGES, meanwhile):
        if parts is not None:
            value = (parts[0] + parts[1].astype(F32)) + (parts[2].astype(F32) + parts[3].astype(F32))
        small = value.astype(BF16)
        parts = [value] + [lax.ppermute(small, "dp", dp_pairs(move)) for move in moves]
        if work is not None:
            parts[3] = after(parts[3], work(small))
    return parts


def parts_over_section(value):
    return [value] + [
        lax.ppermute(value, "section", [(i, (i + k) % 4) for i in range(4)]) for k in (1, 3, 2)
    ]


def parts_to_last_section(value):
    return [value] + [lax.ppermute(value, "section", [(i, 3)]) for i in (2, 0, 1)]


def per_device(
    teacher_logits, prototypes, head_weight, student_out, block_inputs, ln_gain, w_gate, w_up, w_down
):
    packed = lax.all_gather(pack_weights(w_gate[0], w_up[0], w_down[0], 512), "dp", axis=0)
    hidden = w_gate.shape[2]
    shard_rows, down_rows = w_gate.shape[1], w_down.shape[1]

    made = {}

    def make_unit(token):
        made["unit"], made["radius"] = student_unit(after(student_out, token), head_weight)
        return made["unit"]

    early = prototypes.shape[0] // 4

    def first_part(token):
        made["student"], made["p"] = student_products(
            after(made["unit"], token), prototypes, None, 0, early
        )
        return made["student"]

    def second_part(token):
        made["student"], made["p"] = student_products(
            after(made["unit"], token), made["p"], made["student"], early, prototypes.shape[0]
        )
        return made["student"]

    sums, logits = first_column_sums(teacher_logits)
    column_parts = sum_over_dp(sums, (make_unit, first_part))
    sums, weights = row_sums(logits, column_parts)
    sums, weights = column_sums(weights, parts_over_section(sums))
    column_parts = sum_over_dp(sums, (second_part, None))
    sums, weights = row_sums(weights, column_parts)
    student = after(made["student"], sums)
    student = student + lax.ppermute(student, "section", [(1, 2), (0, 3)])
    sums, weights = column_sums(weights, parts_over_section(sums))
    student = after(student, sums)
    student_parts = [student, lax.ppermute(student, "section", [(2, 3)])]
    column_parts = sum_over_dp(sums)
    target = target_products(weights, column_parts, made["p"])
    target_parts = parts_to_last_section(target)

    state = block_forward(after(block_inputs[0], target), ln_gain, packed, shard_rows, hidden)
    unit = after(made["unit"], state[4])
    incoming = head_gradient(student_parts, target_parts, unit, made["radius"], head_weight)

    results = []
    grads = [incoming, incoming]
    for turn in (3, 2, 1, 0):
        for half in (0, 1):
            earlier = results if (turn, half) == (0, 1) else []
            computed, *state = block_backward(grads[half], state, earlier, turn, half, shard_rows, down_rows)
            results.append(computed)
            if turn:
                grads[half] = lax.ppermute(computed, "section", [(turn, turn - 1)])
    return computed[None]


def solution(mesh):
    in_specs = (
        P("dp", "section"),
        P("section", None),
        P(),
        P("dp", None),
        P("section", "dp", None),
        P("section", None),
        P("section", "dp", None),
        P("section", "dp", None),
        P("section", "dp", None),
    )
    out_specs = P("section", "dp", None)
    return jax.shard_map(per_device, mesh=mesh, in_specs=in_specs, out_specs=out_specs, check_vma=False)
```
